512 devices in a mesh: pop: 64 (over y_lo, z, core), shard: 8 (over x, y_hi).
Axes of the slice: x: 4, y: 4 (y_hi: 2, y_lo: 2; y = y_hi * 2 + y_lo), z: 16, core: 2. Of those that a mesh axis runs over, the one named last changes fastest.
Arguments:
- hidden: bfloat16 [8192, 4096], P('pop'), may hold values from -6 to 6
- weight: bfloat16 [4096, 14336], P('pop', 'shard'), may hold values from -0.09375 to 0.09375
- left_factors: bfloat16 [512, 4096], P('pop'), may hold values from -6 to 6
- right_factors: bfloat16 [512, 14336], P('pop', 'shard'), may hold values from -6 to 6
- target: bfloat16 [8192, 14336], P('pop', 'shard'), may hold values from -6 to 6
Outputs:
- up_out: bfloat16 [8192, 14336], P('pop', 'shard')
- step: float32 [4096, 14336], P('pop', 'shard')
- fitness: float32 [512], P('pop')
The draws below stay inside these ranges and needn't reach their ends.
All inputs are finite; a program needn't handle non-finite values.
Results may differ from the reference program's by a relative error of at most 0.001.
Values may be sent and summed in bfloat16 or wider, within the bound.
No kernel may reach another device: no remote copies, remote signals or barrier semaphores. Data moves between devices by JAX's collectives and lax.ppermute only.
A program may use at most 64 MiB of HBM per device.

```python
import math
import jax
import jax.numpy as jnp
from jax import lax

D = 4096
FF = 14336
TOK = 16
MEMBERS = 512
ROWS = 8192


def block_scale(rng, dims, cuts, low, top_value):
    def one(dim, shards_of):
        draws = jax.random.uniform(jax.random.fold_in(jax.random.fold_in(rng, 6), dim), (shards_of,), jnp.float32, low / len(cuts), top_value / len(cuts))
        return jnp.repeat(jnp.exp(draws), dims[dim] // shards_of).reshape((-1,) + (1,) * (len(dims) - dim - 1))

    level = one(*cuts[0])
    for cut in cuts[1:]:
        level = level * one(*cut)
    return level


def bell_draw(own_key, extent, scale, limit, split=(), dtype=jnp.bfloat16):
    array = scale * jax.random.normal(own_key, extent, jnp.float32)
    if split:
        array = array * block_scale(own_key, extent, split, -0.22, 0.18)
    return jnp.clip(array, -limit, limit).astype(dtype)


def setup_inputs(seed: int = 0) -> dict:
    seeds = jax.random.split(jax.random.key(seed), 6)
    hidden = bell_draw(seeds[0], (ROWS, D), 1.0, 6.0, ((0, 64),))
    weight = bell_draw(seeds[1], (D, FF), D ** -0.5, 0.09375, ((0, 64), (1, 8)))
    left_factors = bell_draw(seeds[2], (MEMBERS, D), 1.0, 6.0, ((0, 64),))
    right_factors = bell_draw(seeds[3], (MEMBERS, FF), 1.0, 6.0, ((0, 64), (1, 8)))
    target = bell_draw(seeds[4], (ROWS, FF), 1.0, 6.0, ((0, 64), (1, 8)))
    return {"hidden": hidden, "weight": weight, "left_factors": left_factors, "right_factors": right_factors, "target": target}


noise_scale = 0.5
spread_eps = 1e-05

def reference(hidden, weight, left_factors, right_factors, target):
    base_out = jnp.dot(hidden, weight, preferred_element_type=jnp.float32)
    grouped = hidden.reshape(MEMBERS, TOK, D).astype(jnp.float32)
    projected = jnp.einsum('mtd,md->mt', grouped, left_factors.astype(jnp.float32)) / math.sqrt(D)
    right_wide = right_factors.astype(jnp.float32)
    perturbed = base_out.reshape(MEMBERS, TOK, FF) + noise_scale * projected[:, :, None] * right_wide[:, None, :]
    up_out = perturbed.astype(jnp.bfloat16).reshape(ROWS, FF)
    directions = target.reshape(MEMBERS, TOK, FF).astype(jnp.float32)
    reward = lax.optimization_barrier(jnp.sum(jax.nn.silu(perturbed) * directions, axis=(1, 2)))
    mean_reward = jnp.sum(reward) / MEMBERS
    centered = reward - mean_reward
    spread = jnp.sum(centered * centered) / MEMBERS
    fitness = centered / jnp.sqrt(spread + spread_eps)
    weighted = left_factors.astype(jnp.float32) * fitness[:, None]
    summed = lax.dot_general(weighted, right_wide, (((0,), (0,)), ((), ())), precision=lax.Precision.HIGHEST)
    step = summed / math.sqrt(MEMBERS)
    return (up_out, step, fitness)
```

```python
import math

import jax
import jax.numpy as jnp
from jax import lax
from jax.experimental import pallas as pl
from jax.experimental.pallas import tpu as pltpu
from jax.sharding import Mesh, PartitionSpec as P

noise_scale = 0.5
spread_eps = 1e-05
AXES = ("ylo", "z", "core", "x", "yhi")
SIZES = (2, 16, 2, 4, 2)
SWAP = [(0, 1), (1, 0)]


def project_kernel(gathered, hidden, target, right, projected, up, reward, total):
    i = pl.program_id(0)

    @pl.when(i == 0)
    def _():
        total[...] = jnp.zeros_like(total)

    slabs, _, cols = gathered.shape
    block = gathered[:, :128, :].reshape(slabs * 128, cols)
    total[...] += jnp.dot(hidden[...], block, preferred_element_type=jnp.float32)

    @pl.when(i == pl.num_programs(0) - 1)
    def _():
        rows = total.shape[0]
        members = right.shape[0]
        tokens = rows // members
        base = total[...].reshape(members, tokens, cols)
        factor = right[...].astype(jnp.float32)
        value = base + projected[...].reshape(members, tokens, 1) * factor[:, None, :]
        up[...] = value.reshape(rows, cols).astype(jnp.bfloat16)
        aim = target[...].astype(jnp.float32).reshape(members, tokens, cols)
        gain = value / (1.0 + jnp.exp(-value)) * aim
        summed = jnp.sum(jnp.sum(gain, axis=1), axis=-1, keepdims=True)
        reward[...] = jnp.broadcast_to(summed, reward.shape)


def project(gathered, hidden, target, right, projected):
    blocks, depth, cols = gathered.shape
    rows = hidden.shape[0]
    members = right.shape[0]
    slabs = 4
    whole = lambda *shape: pl.BlockSpec(shape, lambda i: (0,) * len(shape))
    return pl.pallas_call(
        project_kernel,
        grid=(blocks // slabs,),
        in_specs=[
            pl.BlockSpec((slabs, depth, cols), lambda i: (i, 0, 0)),
            pl.BlockSpec((rows, slabs * 128), lambda i: (0, i)),
            whole(rows, cols),
            whole(members, cols),
            whole(rows, 1),
        ],
        out_specs=[whole(rows, cols), whole(members, 128)],
        out_shape=[
            jax.ShapeDtypeStruct((rows, cols), jnp.bfloat16),
            jax.ShapeDtypeStruct((members, 128), jnp.float32),
        ],
        scratch_shapes=[pltpu.VMEM((rows, cols), jnp.float32)],
        compiler_params=pltpu.CompilerParams(vmem_limit_bytes=40 * 1024 * 1024),
        cost_estimate=pl.CostEstimate(
            flops=2 * rows * blocks * 128 * cols,
            bytes_accessed=blocks * depth * cols * 2,
            transcendentals=rows * cols,
        ),
    )(gathered, hidden, target, right, projected)


def step_kernel(left, fitness, right, out):
    weighted = left[...].astype(jnp.float32) * fitness[...]
    high = weighted.astype(jnp.bfloat16)
    low = (weighted - high.astype(jnp.float32)).astype(jnp.bfloat16)
    both = jnp.concatenate([high, low], axis=0)
    product = jnp.dot(both, right[...], preferred_element_type=jnp.float32)
    rows = left.shape[0]
    out[...] = (product[:rows] + product[rows:]) * (1.0 / math.sqrt(left.shape[1]))


def step_product(left, fitness, right):
    rows, members = left.shape
    cols = right.shape[1]
    width = 256
    return pl.pallas_call(
        step_kernel,
        grid=(cols // width,),
        in_specs=[
            pl.BlockSpec((rows, members), lambda j: (0, 0)),
            pl.BlockSpec((1, members), lambda j: (0, 0)),
            pl.BlockSpec((members, width), lambda j: (0, j)),
        ],
        out_specs=pl.BlockSpec((rows, width), lambda j: (0, j)),
        out_shape=jax.ShapeDtypeStruct((rows, cols), jnp.float32),
        compiler_params=pltpu.CompilerParams(vmem_limit_bytes=40 * 1024 * 1024),
        cost_estimate=pl.CostEstimate(
            flops=4 * rows * members * cols,
            bytes_accessed=members * cols * 2 + rows * cols * 4,
            transcendentals=0,
        ),
    )(left, fitness, right)


def local(hidden, weight, left_factors, right_factors, target):
    members, features = left_factors.shape
    rows = hidden.shape[0]
    tokens = rows // members
    depth, cols = weight.shape
    half = cols // 2
    ylo = lax.axis_index("ylo")
    z = lax.axis_index("z")
    core = lax.axis_index("core")

    def own(a):
        return lax.dynamic_slice_in_dim(a, ylo * half, half, axis=1)

    def other(a):
        return lax.dynamic_slice_in_dim(a, (1 - ylo) * half, half, axis=1)

    slab = jnp.concatenate([weight, right_factors], axis=0)
    slab_own = own(slab)
    slab_recv = lax.ppermute(other(slab), "ylo", SWAP)
    right_local = jnp.concatenate([slab_own[depth:], slab_recv[depth:]], axis=0)
    packed = jnp.concatenate([slab_own[:depth], slab_recv[:depth], right_local], axis=0)
    gathered = lax.all_gather(packed, ("z", "core"), axis=0, tiled=False)

    after, hidden_b, left_b, target_b = lax.optimization_barrier(
        (packed, hidden, left_factors, target)
    )
    rows_recv = lax.ppermute(hidden_b, "ylo", SWAP)
    target_recv = lax.ppermute(other(target_b), "ylo", SWAP)
    projected_own = (
        jnp.einsum(
            "mtd,md->mt",
            hidden_b.reshape(members, tokens, features),
            left_b,
            preferred_element_type=jnp.float32,
        ).reshape(rows, 1)
        * (noise_scale / math.sqrt(features))
    )
    projected_recv = lax.ppermute(projected_own, "ylo", SWAP)
    projected = jnp.concatenate([projected_own, projected_recv], axis=0)
    target_all = jnp.concatenate([own(target_b), target_recv], axis=0)
    hidden_all = jnp.concatenate([hidden_b, rows_recv], axis=0)
    spread_rows = hidden_all.reshape(2 * rows, 2, features // (2 * depth), depth)
    spread_rows = jnp.where(ylo == 0, spread_rows, spread_rows[:, ::-1])
    hidden_all = spread_rows.transpose(0, 2, 1, 3).reshape(2 * rows, features)

    left_split = left_b.reshape(members, features // depth, depth).transpose(1, 0, 2)
    left_all = lax.all_to_all(left_split, ("ylo", "z", "core"), 0, 0, tiled=True)
    left_all = left_all.reshape(2, features // (2 * depth), members, depth)
    left_all = jnp.where(ylo == 0, left_all, left_all[::-1])
    left_all = left_all.transpose(3, 1, 0, 2).reshape(depth, -1)

    up, reward_rows = project(gathered, hidden_all, target_all, right_local, projected)

    up_recv = lax.ppermute(up[rows:], "ylo", SWAP)
    up_own = up[:rows]
    up_out = jnp.where(
        ylo == 0,
        jnp.concatenate([up_own, up_recv], axis=1),
        jnp.concatenate([up_recv, up_own], axis=1),
    )
    portion = gathered[:, 2 * depth :]
    portion_recv = lax.ppermute(
        jnp.concatenate([portion[:, members:], portion[:, :members]], axis=1), "ylo", SWAP
    )
    portion = portion.reshape(-1, half)
    portion_recv = portion_recv.reshape(-1, half)
    right_all = jnp.where(
        ylo == 0,
        jnp.concatenate([portion, portion_recv], axis=1),
        jnp.concatenate([portion_recv, portion], axis=1),
    )

    part = reward_rows[:, 0].reshape(2, members)
    part = jnp.where(ylo == 0, part, part[::-1]).reshape(1, 2 * members)
    near = lax.all_to_all(
        jnp.broadcast_to(part, (32, 2 * members)), ("ylo", "core", "x", "yhi"), 0, 0, tiled=True
    )
    near = near.reshape(2, 2, 8, 2 * members).sum(axis=(0, 2)).reshape(1, 4 * members)
    reward = lax.all_to_all(jnp.broadcast_to(near, (16, 4 * members)), "z", 0, 0, tiled=True)
    reward = reward.reshape(-1)
    count = reward.shape[0]
    centered = reward - jnp.sum(reward) / count
    spread = jnp.sum(centered * centered) / count
    fitness_all = (centered / jnp.sqrt(spread + spread_eps)).reshape(16, 2, 2, members)
    fitness = lax.dynamic_slice(fitness_all, (z, core, ylo, 0), (1, 1, 1, members)).reshape(members)
    fitness_order = jnp.where(ylo == 0, fitness_all, fitness_all[:, :, ::-1]).reshape(1, count)

    step = step_product(left_all, fitness_order, right_all)
    return (up_out, step, fitness)


def solution(mesh):
    fine = Mesh(mesh.devices.reshape(SIZES), AXES)
    pop = ("ylo", "z", "core")
    shard = ("x", "yhi")
    in_specs = (P(pop, None), P(pop, shard), P(pop, None), P(pop, shard), P(pop, shard))
    out_specs = (P(pop, shard), P(pop, shard), P(pop))
    return jax.shard_map(local, mesh=fine, in_specs=in_specs, out_specs=out_specs, check_vma=False)
```

```python
import math

import jax
import jax.numpy as jnp
from jax import lax
from jax.experimental import pallas as pl
from jax.experimental.pallas import tpu as pltpu
from jax.sharding import Mesh, PartitionSpec as P

noise_scale = 0.5
spread_eps = 1e-05
AXES = ("ylo", "z", "core", "x", "yhi")
SIZES = (2, 16, 2, 4, 2)
SWAP = [(0, 1), (1, 0)]


def project_kernel(gathered, hidden, target, right, projected, up, reward, total):
    i = pl.program_id(0)
    slabs, _, cols = gathered.shape
    block = gathered[:, :128, :].reshape(slabs * 128, cols)
    part = jnp.dot(hidden[...], block, preferred_element_type=jnp.float32)

    @pl.when(i == 0)
    def _():
        total[...] = part

    @pl.when(i > 0)
    def _():
        total[...] += part

    @pl.when(i == pl.num_programs(0) - 1)
    def _():
        rows = total.shape[0]
        members = right.shape[0]
        tokens = rows // members
        base = total[...].reshape(members, tokens, cols)
        factor = right[...].astype(jnp.float32)
        value = base + projected[...].reshape(members, tokens, 1) * factor[:, None, :]
        up[...] = value.reshape(rows, cols).astype(jnp.bfloat16)
        aim = target[...].astype(jnp.float32).reshape(members, tokens, cols)
        gain = value * (0.5 + 0.5 * jnp.tanh(0.5 * value)) * aim
        summed = jnp.sum(jnp.sum(gain, axis=1), axis=-1, keepdims=True)
        peers = reward.shape[0]
        lanes = reward.shape[-1]
        spot = lax.broadcasted_iota(jnp.int32, (members, lanes), 0) == lax.broadcasted_iota(
            jnp.int32, (members, lanes), 1
        )
        line = jnp.sum(jnp.where(spot, summed, 0.0), axis=0, keepdims=True)
        reward[...] = jnp.broadcast_to(line[None], reward.shape)


def project(gathered, hidden, target, right, projected, peers):
    blocks, depth, cols = gathered.shape
    rows = hidden.shape[0]
    members = right.shape[0]
    slabs = 4
    whole = lambda *shape: pl.BlockSpec(shape, lambda i: (0,) * len(shape))
    return pl.pallas_call(
        project_kernel,
        grid=(blocks // slabs,),
        in_specs=[
            pl.BlockSpec((slabs, depth, cols), lambda i: (i, 0, 0)),
            pl.BlockSpec((rows, slabs * 128), lambda i: (0, i)),
            whole(rows, cols),
            whole(members, cols),
            whole(rows, 1),
        ],
        out_specs=[whole(rows, cols), whole(peers, 1, members)],
        out_shape=[
            jax.ShapeDtypeStruct((rows, cols), jnp.bfloat16),
            jax.ShapeDtypeStruct((peers, 1, members), jnp.float32),
        ],
        scratch_shapes=[pltpu.VMEM((rows, cols), jnp.float32)],
        compiler_params=pltpu.CompilerParams(vmem_limit_bytes=60 * 1024 * 1024),
        cost_estimate=pl.CostEstimate(
            flops=2 * rows * blocks * 128 * cols,
            bytes_accessed=blocks * depth * cols * 2,
            transcendentals=rows * cols,
        ),
    )(gathered, hidden, target, right, projected)


def step_kernel(place, reward, left, right_own, right_other, out, fitness, both):
    h = pl.program_id(0)
    members, depth = left.shape
    blocks, lanes = reward.shape[0], reward.shape[2]

    @pl.when(h == 0)
    def _():
        value = reward[...].reshape(blocks, lanes)
        total = jnp.sum(jnp.sum(value, axis=0, keepdims=True), axis=1, keepdims=True)
        centered = value - total * (1.0 / members)
        squares = jnp.sum(jnp.sum(centered * centered, axis=0, keepdims=True), axis=1, keepdims=True)
        score = centered / jnp.sqrt(squares * (1.0 / members) + spread_eps)
        shape = (blocks, lanes, lanes)
        spot = lax.broadcasted_iota(jnp.int32, shape, 1) == lax.broadcasted_iota(jnp.int32, shape, 2)
        column = jnp.sum(jnp.where(spot, score[:, None, :], 0.0), axis=-1, keepdims=True)
        column = column.reshape(members, 1)
        own = fitness.shape[1]
        pick = (members, own)
        mine = lax.broadcasted_iota(jnp.int32, pick, 0) == (
            lax.broadcasted_iota(jnp.int32, pick, 1) + place[1]
        )
        fitness[...] = jnp.sum(jnp.where(mine, column, 0.0), axis=0, keepdims=True)
        weighted = left[...].astype(jnp.float32) * column
        high = weighted.astype(jnp.bfloat16)
        low = (weighted - high.astype(jnp.float32)).astype(jnp.bfloat16)
        both[...] = jnp.concatenate([high, low], axis=1)

    def multiply(right):
        product = lax.dot_general(
            both[...],
            right[...].reshape(members, right.shape[-1]),
            (((0,), (0,)), ((), ())),
            preferred_element_type=jnp.float32,
        )
        out[...] = (product[:depth] + product[depth:]) * (1.0 / math.sqrt(members))

    @pl.when(h == 0)
    def _():
        multiply(right_own)

    @pl.when(h == 1)
    def _():
        multiply(right_other)


def step_product(place, reward, left, gathered, right_other, own):
    members, depth = left.shape
    blocks, rows, half = gathered.shape
    count = right_other.shape[1]
    return pl.pallas_call(
        step_kernel,
        grid_spec=pltpu.PrefetchScalarGridSpec(
            num_scalar_prefetch=1,
            grid=(2,),
            in_specs=[
                pl.BlockSpec(reward.shape, lambda h, p: (0, 0, 0)),
                pl.BlockSpec((members, depth), lambda h, p: (0, 0)),
                pl.BlockSpec((blocks, count, half), lambda h, p: (0, rows // count - 1, 0)),
                pl.BlockSpec((blocks, count, half), lambda h, p: (0, 0, 0)),
            ],
            out_specs=[
                pl.BlockSpec((depth, half), lambda h, p: (0, (p[0] + h) % 2)),
                pl.BlockSpec((1, own), lambda h, p: (0, 0)),
            ],
            scratch_shapes=[pltpu.VMEM((members, 2 * depth), jnp.bfloat16)],
        ),
        out_shape=[
            jax.ShapeDtypeStruct((depth, 2 * half), jnp.float32),
            jax.ShapeDtypeStruct((1, own), jnp.float32),
        ],
        compiler_params=pltpu.CompilerParams(vmem_limit_bytes=60 * 1024 * 1024),
        cost_estimate=pl.CostEstimate(
            flops=8 * depth * members * half,
            bytes_accessed=members * half * 4 + depth * half * 8,
            transcendentals=0,
        ),
    )(place, reward, left, gathered, right_other)


def local(hidden, weight, left_factors, right_factors, target):
    members, features = left_factors.shape
    rows = hidden.shape[0]
    tokens = rows // members
    depth, cols = weight.shape
    half = cols // 2
    ylo = lax.axis_index("ylo")
    z = lax.axis_index("z")
    core = lax.axis_index("core")
    low = ylo == 0

    def own(a):
        return jnp.where(low, a[:, :half], a[:, half:])

    def other(a):
        return jnp.where(low, a[:, half:], a[:, :half])

    def order(a, b, axis=0):
        return jnp.where(
            low, jnp.concatenate([a, b], axis=axis), jnp.concatenate([b, a], axis=axis)
        )

    mine, sent = own(right_factors), other(right_factors)
    slab_recv = lax.ppermute(
        jnp.concatenate([other(weight), sent, mine], axis=0), "ylo", SWAP
    )
    theirs, theirs_far = slab_recv[depth : depth + members], slab_recv[depth + members :]
    right_local = order(mine, theirs)
    packed = jnp.concatenate([order(own(weight), slab_recv[:depth]), right_local], axis=0)
    gathered = lax.all_gather(packed, ("z", "core"), axis=0, tiled=False)

    after, hidden_b, left_b, target_b, sent, theirs_far = lax.optimization_barrier(
        (packed, hidden, left_factors, target, sent, theirs_far)
    )
    rows_recv = lax.ppermute(hidden_b, "ylo", SWAP)
    target_recv = lax.ppermute(other(target_b), "ylo", SWAP)
    projected_own = (
        jnp.einsum(
            "mtd,md->mt",
            hidden_b.reshape(members, tokens, features),
            left_b,
            preferred_element_type=jnp.float32,
        ).reshape(rows, 1)
        * (noise_scale / math.sqrt(features))
    )
    projected_recv = lax.ppermute(projected_own, "ylo", SWAP)
    projected = order(projected_own, projected_recv)
    target_all = order(own(target_b), target_recv)
    hidden_all = order(hidden_b, rows_recv)
    spread_rows = hidden_all.reshape(2 * rows, 2, features // (2 * depth), depth)
    hidden_all = spread_rows.transpose(0, 2, 1, 3).reshape(2 * rows, features)

    left_split = left_b.reshape(members, features // depth, depth).transpose(1, 0, 2)
    left_all = lax.all_to_all(left_split, ("ylo", "z", "core"), 0, 0, tiled=True)
    left_all = left_all.reshape(2, features // (2 * depth), members, depth)
    left_all = left_all.transpose(1, 0, 2, 3).reshape(-1, depth)
    far = order(sent, theirs_far)
    right_other = lax.all_gather(far, ("z", "core"), axis=0, tiled=False)

    hidden_all, left_all, right_other = lax.optimization_barrier((hidden_all, left_all, right_other))
    up, part = project(gathered, hidden_all, target_all, right_local, projected, 32)

    near = lax.all_to_all(part, ("ylo", "core", "x", "yhi"), 0, 0, tiled=True)
    near = near.reshape(2, 2, 8, 2 * members).sum(axis=(0, 2))
    near = near.reshape(1, 1, 4 * members)
    reward = lax.all_to_all(jnp.broadcast_to(near, (16, 1, 4 * members)), "z", 0, 0, tiled=True)

    up_recv = lax.ppermute(jnp.where(low, up[rows:], up[:rows]), "ylo", SWAP)
    up_out = order(jnp.where(low, up[:rows], up[rows:]), up_recv, axis=1)

    place = jnp.stack([ylo, z * 4 * members + core * 2 * members + ylo * members]).astype(jnp.int32)
    step, fitness = step_product(place, reward, left_all, gathered, right_other, members)
    return (up_out, step, fitness.reshape(members))


def solution(mesh):
    fine = Mesh(mesh.devices.reshape(SIZES), AXES)
    pop = ("ylo", "z", "core")
    shard = ("x", "yhi")
    in_specs = (P(pop, None), P(pop, shard), P(pop, None), P(pop, shard), P(pop, shard))
    out_specs = (P(pop, shard), P(pop, shard), P(pop))
    return jax.shard_map(local, mesh=fine, in_specs=in_specs, out_specs=out_specs, check_vma=False)
```

```python
import math

import jax
import jax.numpy as jnp
from jax import lax
from jax.experimental import pallas as pl
from jax.experimental.pallas import tpu as pltpu
from jax.sharding import Mesh, PartitionSpec as P

noise_scale = 0.5
spread_eps = 1e-05
AXES = ("ylo", "z", "core", "x", "yhi")
SIZES = (2, 16, 2, 4, 2)
SWAP = [(0, 1), (1, 0)]


def project_kernel(
    place, gathered, hidden, target, right, projected, keep, send, reward, portion, total, held, sems
):
    chunks, slabs, width, cols = held.shape
    copies = []
    for i in range(chunks):
        copy = pltpu.make_async_copy(
            gathered.at[pl.ds(i * slabs, slabs), pl.ds(0, width), :], held.at[i], sems.at[i]
        )
        copy.start()
        copies.append(copy)
    last = pltpu.make_async_copy(
        gathered.at[:, pl.ds(width, portion.shape[1]), :], portion, sems.at[chunks]
    )
    last.start()
    span = slabs * width
    for i in range(chunks):
        copies[i].wait()
        part = jnp.dot(
            hidden[:, i * span : (i + 1) * span],
            held[i].reshape(span, cols),
            preferred_element_type=jnp.float32,
        )
        if i == 0:
            total[...] = part
        else:
            total[...] += part
    rows = total.shape[0]
    members = right.shape[0]
    tokens = rows // members
    base = total[...].reshape(members, tokens, cols)
    factor = right[...].astype(jnp.float32)
    value = base + projected[...].reshape(members, tokens, 1) * factor[:, None, :]
    up = value.reshape(rows, cols).astype(jnp.bfloat16)
    keep[...] = up[: rows // 2]
    send[...] = up[rows // 2 :]
    aim = target[...].astype(jnp.float32).reshape(members, tokens, cols)
    gain = value * (0.5 + 0.5 * jnp.tanh(0.5 * value)) * aim
    summed = jnp.sum(jnp.sum(gain, axis=1), axis=-1, keepdims=True)
    shape = (members, reward.shape[-1])
    row = lax.broadcasted_iota(jnp.int32, shape, 0) + place[0] * (members // 2)
    row = jnp.where(row < members, row, row - members)
    spot = row == lax.broadcasted_iota(jnp.int32, shape, 1)
    line = jnp.sum(jnp.where(spot, summed, 0.0), axis=0, keepdims=True)
    reward[...] = jnp.broadcast_to(line[None], reward.shape)
    last.wait()


VMEM = pl.BlockSpec(memory_space=pltpu.VMEM)
SMEM = pl.BlockSpec(memory_space=pltpu.SMEM)
ANY = pl.BlockSpec(memory_space=pl.ANY)


def project(place, gathered, hidden, target, right, projected, peers):
    blocks, depth, cols = gathered.shape
    rows, features = hidden.shape
    members = right.shape[0]
    slabs = 4
    width = features // blocks
    return pl.pallas_call(
        project_kernel,
        in_specs=[SMEM, ANY, VMEM, VMEM, VMEM, VMEM],
        out_specs=[VMEM, VMEM, VMEM, VMEM],
        out_shape=[
            jax.ShapeDtypeStruct((rows // 2, cols), jnp.bfloat16),
            jax.ShapeDtypeStruct((rows // 2, cols), jnp.bfloat16),
            jax.ShapeDtypeStruct((peers, 1, members), jnp.float32),
            jax.ShapeDtypeStruct((blocks, depth - width, cols), jnp.bfloat16),
        ],
        scratch_shapes=[
            pltpu.VMEM((rows, cols), jnp.float32),
            pltpu.VMEM((blocks // slabs, slabs, width, cols), jnp.bfloat16),
            pltpu.SemaphoreType.DMA((blocks // slabs + 1,)),
        ],
        compiler_params=pltpu.CompilerParams(vmem_limit_bytes=53 * 1024 * 1024),
        cost_estimate=pl.CostEstimate(
            flops=2 * rows * features * cols,
            bytes_accessed=features * cols * 2,
            transcendentals=rows * cols,
        ),
    )(place, gathered, hidden, target, right, projected)


def step_kernel(place, reward, left, right_own, right_other, keep, recv, out, up, fitness):
    members, depth = left.shape
    blocks, _, lanes = reward.shape
    half = right_own.shape[2]
    own_at = pl.multiple_of(place[0] * half, 128)
    other_at = pl.multiple_of((1 - place[0]) * half, 128)
    up[:, pl.ds(own_at, half)] = keep[...]
    up[:, pl.ds(other_at, half)] = recv[...]
    value = reward[...].reshape(blocks, lanes)
    total = jnp.sum(jnp.sum(value, axis=0, keepdims=True), axis=1, keepdims=True)
    centered = value - total * (1.0 / members)
    squares = jnp.sum(jnp.sum(centered * centered, axis=0, keepdims=True), axis=1, keepdims=True)
    score = centered / jnp.sqrt(squares * (1.0 / members) + spread_eps)
    shape = (blocks, lanes, lanes)
    spot = lax.broadcasted_iota(jnp.int32, shape, 1) == lax.broadcasted_iota(jnp.int32, shape, 2)
    column = jnp.sum(jnp.where(spot, score[:, None, :], 0.0), axis=-1, keepdims=True)
    column = column.reshape(members, 1)
    pick = (members, fitness.shape[1])
    mine = lax.broadcasted_iota(jnp.int32, pick, 0) == (
        lax.broadcasted_iota(jnp.int32, pick, 1) + place[1]
    )
    fitness[...] = jnp.sum(jnp.where(mine, column, 0.0), axis=0, keepdims=True)
    weighted = left[...].astype(jnp.float32) * column
    high = weighted.astype(jnp.bfloat16)
    low = (weighted - high.astype(jnp.float32)).astype(jnp.bfloat16)
    both = jnp.concatenate([high, low], axis=1)

    def multiply(right, at):
        product = lax.dot_general(
            both,
            right.reshape(members, half),
            (((0,), (0,)), ((), ())),
            preferred_element_type=jnp.float32,
        )
        out[:, pl.ds(at, half)] = (product[:depth] + product[depth:]) * (1.0 / math.sqrt(members))

    multiply(right_other[...], other_at)
    multiply(right_own[...], own_at)


def step_product(place, reward, left, right_own, right_other, keep, recv, own):
    members, depth = left.shape
    half = right_other.shape[2]
    return pl.pallas_call(
        step_kernel,
        in_specs=[SMEM, VMEM, VMEM, VMEM, VMEM, VMEM, VMEM],
        out_specs=[VMEM, VMEM, VMEM],
        out_shape=[
            jax.ShapeDtypeStruct((depth, 2 * half), jnp.float32),
            jax.ShapeDtypeStruct((keep.shape[0], 2 * half), jnp.bfloat16),
            jax.ShapeDtypeStruct((1, own), jnp.float32),
        ],
        compiler_params=pltpu.CompilerParams(vmem_limit_bytes=24 * 1024 * 1024),
        cost_estimate=pl.CostEstimate(
            flops=8 * depth * members * half,
            bytes_accessed=members * half * 4 + depth * half * 8,
            transcendentals=0,
        ),
    )(place, reward, left, right_own, right_other, keep, recv)


def local(hidden, weight, left_factors, right_factors, target):
    members, features = left_factors.shape
    rows = hidden.shape[0]
    tokens = rows // members
    depth, cols = weight.shape
    half = cols // 2
    ylo = lax.axis_index("ylo")
    z = lax.axis_index("z")
    core = lax.axis_index("core")
    low = ylo == 0

    def own(a):
        return jnp.where(low, a[:, :half], a[:, half:])

    def other(a):
        return jnp.where(low, a[:, half:], a[:, :half])

    def order(a, b, axis=0):
        return jnp.where(
            low, jnp.concatenate([a, b], axis=axis), jnp.concatenate([b, a], axis=axis)
        )

    mine, sent = own(right_factors), other(right_factors)
    slab_recv = lax.ppermute(
        jnp.concatenate([other(weight), sent, mine], axis=0), "ylo", SWAP
    )
    theirs, theirs_far = slab_recv[depth : depth + members], slab_recv[depth + members :]
    right_local = jnp.concatenate([mine, theirs], axis=0)
    packed = jnp.concatenate(
        [order(own(weight), slab_recv[:depth]), order(mine, theirs)], axis=0
    )
    gathered = lax.all_gather(packed, ("z", "core"), axis=0, tiled=False)

    after, hidden_b, left_b, target_b, sent, theirs_far = lax.optimization_barrier(
        (packed, hidden, left_factors, target, sent, theirs_far)
    )
    rows_recv = lax.ppermute(hidden_b, "ylo", SWAP)
    target_recv = lax.ppermute(other(target_b), "ylo", SWAP)
    projected_own = (
        jnp.einsum(
            "mtd,md->mt",
            hidden_b.reshape(members, tokens, features),
            left_b,
            preferred_element_type=jnp.float32,
        ).reshape(rows, 1)
        * (noise_scale / math.sqrt(features))
    )
    projected_recv = lax.ppermute(projected_own, "ylo", SWAP)
    projected = jnp.concatenate([projected_own, projected_recv], axis=0)
    target_all = jnp.concatenate([own(target_b), target_recv], axis=0)
    hidden_all = jnp.concatenate([hidden_b, rows_recv], axis=0)
    spread_rows = hidden_all.reshape(2 * rows, 2, features // (2 * depth), depth)
    hidden_all = spread_rows.transpose(0, 2, 1, 3).reshape(2 * rows, features)

    left_split = left_b.reshape(members, features // depth, depth).transpose(1, 0, 2)
    left_all = lax.all_to_all(left_split, ("ylo", "z", "core"), 0, 0, tiled=True)
    left_all = left_all.reshape(2, features // (2 * depth), members, depth)
    left_all = left_all.transpose(1, 0, 2, 3).reshape(-1, depth)
    far = order(sent, theirs_far)
    right_other = lax.all_gather(far, ("z", "core"), axis=0, tiled=False)

    hidden_all, left_all, right_other = lax.optimization_barrier((hidden_all, left_all, right_other))
    place = jnp.stack([ylo, z * 4 * members + core * 2 * members + ylo * members]).astype(jnp.int32)
    keep, send, part, right_own = project(
        place, gathered, hidden_all, target_all, right_local, projected, 32
    )

    near = lax.all_to_all(part, ("ylo", "core", "x", "yhi"), 0, 0, tiled=True)
    near, send = lax.optimization_barrier((near, send))
    recv = lax.ppermute(send, "ylo", SWAP)
    near = near.reshape(2, 2, 8, 2 * members).sum(axis=(0, 2)).reshape(1, 1, 4 * members)
    reward = lax.all_to_all(jnp.broadcast_to(near, (16, 1, 4 * members)), "z", 0, 0, tiled=True)

    step, up_out, fitness = step_product(
        place, reward, left_all, right_own, right_other, keep, recv, members
    )
    return (up_out, step, fitness.reshape(members))


def solution(mesh):
    fine = Mesh(mesh.devices.reshape(SIZES), AXES)
    pop = ("ylo", "z", "core")
    shard = ("x", "yhi")
    in_specs = (P(pop, None), P(pop, shard), P(pop, None), P(pop, shard), P(pop, shard))
    out_specs = (P(pop, shard), P(pop, shard), P(pop))
    return jax.shard_map(local, mesh=fine, in_specs=in_specs, out_specs=out_specs, check_vma=False)
```

```python
import math

import jax
import jax.numpy as jnp
from jax import lax
from jax.experimental import pallas as pl
from jax.experimental.pallas import tpu as pltpu
from jax.sharding import Mesh, PartitionSpec as P

noise_scale = 0.5
spread_eps = 1e-05
AXES = ("ylo", "z", "core", "x", "yhi")
SIZES = (2, 16, 2, 4, 2)
SWAP = [(0, 1), (1, 0)]


def project_kernel(
    place, gathered, hidden_hbm, target_hbm, right, projected, keep, send, reward, held, hidden, target, sems
):
    blocks, width, _ = held.shape[1:]
    cols = target.shape[1]
    rows, features = hidden.shape
    load_hidden = pltpu.make_async_copy(hidden_hbm, hidden, sems.at[0])
    load_hidden.start()
    members = right.shape[0]
    tokens = rows // members
    spans = column_spans(cols)
    copies = []
    for i, (at, size) in enumerate(spans):
        copy = pltpu.make_async_copy(
            gathered.at[:, pl.ds(0, width), pl.ds(at, size)],
            held.at[i, :, :, pl.ds(0, size)],
            sems.at[2 + i],
        )
        copy.start()
        copies.append(copy)
        if i == 0:
            load_target = pltpu.make_async_copy(target_hbm, target, sems.at[1])
            load_target.start()
    scale = projected[...].reshape(members, tokens, 1)
    summed = jnp.zeros((members, 1), jnp.float32)
    load_hidden.wait()
    for i, (at, size) in enumerate(spans):
        copies[i].wait()
        if i == 0:
            load_target.wait()
        base = jnp.dot(
            hidden[...],
            held[i, :, :, :size].reshape(features, size),
            preferred_element_type=jnp.float32,
        ).reshape(members, tokens, size)
        factor = right[:, at : at + size].astype(jnp.float32)
        value = base + scale * factor[:, None, :]
        up = value.reshape(rows, size).astype(jnp.bfloat16)
        keep[:, at : at + size] = up[: rows // 2]
        send[:, at : at + size] = up[rows // 2 :]
        aim = target[:, at : at + size].astype(jnp.float32).reshape(members, tokens, size)
        gain = value * (0.5 + 0.5 * jnp.tanh(0.5 * value)) * aim
        summed += jnp.sum(jnp.sum(gain, axis=1), axis=-1, keepdims=True)
    shape = (members, reward.shape[-1])
    row = lax.broadcasted_iota(jnp.int32, shape, 0) + place[0] * (members // 2)
    row = jnp.where(row < members, row, row - members)
    spot = row == lax.broadcasted_iota(jnp.int32, shape, 1)
    line = jnp.sum(jnp.where(spot, summed, 0.0), axis=0, keepdims=True)
    reward[...] = jnp.broadcast_to(line[None], reward.shape)


def column_spans(cols, size=256):
    return [(at, min(size, cols - at)) for at in range(0, cols, size)]


ANY = pl.BlockSpec(memory_space=pl.ANY)
VMEM = pl.BlockSpec(memory_space=pltpu.VMEM)
SMEM = pl.BlockSpec(memory_space=pltpu.SMEM)


def project(place, gathered, hidden, target, right, projected, peers):
    blocks, _, cols = gathered.shape
    rows, features = hidden.shape
    members = right.shape[0]
    width = features // blocks
    spans = column_spans(cols)
    return pl.pallas_call(
        project_kernel,
        in_specs=[SMEM, ANY, ANY, ANY, VMEM, VMEM],
        out_specs=[VMEM, VMEM, VMEM],
        out_shape=[
            jax.ShapeDtypeStruct((rows // 2, cols), jnp.bfloat16),
            jax.ShapeDtypeStruct((rows // 2, cols), jnp.bfloat16),
            jax.ShapeDtypeStruct((peers, 1, members), jnp.float32),
        ],
        scratch_shapes=[
            pltpu.VMEM((len(spans), blocks, width, spans[0][1]), jnp.bfloat16),
            pltpu.VMEM(hidden.shape, jnp.bfloat16),
            pltpu.VMEM(target.shape, jnp.bfloat16),
            pltpu.SemaphoreType.DMA((len(spans) + 2,)),
        ],
        compiler_params=pltpu.CompilerParams(vmem_limit_bytes=53 * 1024 * 1024),
        cost_estimate=pl.CostEstimate(
            flops=2 * rows * features * cols,
            bytes_accessed=features * cols * 2,
            transcendentals=rows * cols,
        ),
    )(place, gathered, hidden, target, right, projected)


def step_kernel(place, reward, left, gathered, right_other, out, fitness, right_own, sem):
    count = right_own.shape[1]
    copy = pltpu.make_async_copy(
        gathered.at[:, pl.ds(gathered.shape[1] - count, count), :], right_own, sem
    )
    copy.start()
    members, depth = left.shape
    blocks, _, lanes = reward.shape
    half = right_own.shape[2]
    own_at = pl.multiple_of(place[0] * half, 128)
    other_at = pl.multiple_of((1 - place[0]) * half, 128)
    value = reward[...].reshape(blocks, lanes)
    total = jnp.sum(jnp.sum(value, axis=0, keepdims=True), axis=1, keepdims=True)
    centered = value - total * (1.0 / members)
    squares = jnp.sum(jnp.sum(centered * centered, axis=0, keepdims=True), axis=1, keepdims=True)
    score = centered / jnp.sqrt(squares * (1.0 / members) + spread_eps)
    shape = (blocks, lanes, lanes)
    spot = lax.broadcasted_iota(jnp.int32, shape, 1) == lax.broadcasted_iota(jnp.int32, shape, 2)
    column = jnp.sum(jnp.where(spot, score[:, None, :], 0.0), axis=-1, keepdims=True)
    column = column.reshape(members, 1)
    pick = (members, fitness.shape[1])
    mine = lax.broadcasted_iota(jnp.int32, pick, 0) == (
        lax.broadcasted_iota(jnp.int32, pick, 1) + place[1]
    )
    fitness[...] = jnp.sum(jnp.where(mine, column, 0.0), axis=0, keepdims=True)
    weighted = left[...].astype(jnp.float32) * column
    high = weighted.astype(jnp.bfloat16)
    low = (weighted - high.astype(jnp.float32)).astype(jnp.bfloat16)
    both = jnp.concatenate([high, low], axis=1)

    def multiply(right, at):
        product = lax.dot_general(
            both,
            right.reshape(members, half),
            (((0,), (0,)), ((), ())),
            preferred_element_type=jnp.float32,
        )
        out[:, pl.ds(at, half)] = (product[:depth] + product[depth:]) * (1.0 / math.sqrt(members))

    multiply(right_other[...], other_at)
    copy.wait()
    multiply(right_own[...], own_at)


def step_product(place, reward, left, gathered, right_other, own):
    members, depth = left.shape
    half = right_other.shape[2]
    return pl.pallas_call(
        step_kernel,
        in_specs=[SMEM, VMEM, VMEM, ANY, VMEM],
        out_specs=[VMEM, VMEM],
        out_shape=[
            jax.ShapeDtypeStruct((depth, 2 * half), jnp.float32),
            jax.ShapeDtypeStruct((1, own), jnp.float32),
        ],
        scratch_shapes=[
            pltpu.VMEM(right_other.shape, jnp.bfloat16),
            pltpu.SemaphoreType.DMA,
        ],
        compiler_params=pltpu.CompilerParams(vmem_limit_bytes=53 * 1024 * 1024),
        cost_estimate=pl.CostEstimate(
            flops=128 * depth * members * half,
            bytes_accessed=members * half * 4 + depth * half * 8,
            transcendentals=0,
        ),
    )(place, reward, left, gathered, right_other)


def local(hidden, weight, left_factors, right_factors, target):
    members, features = left_factors.shape
    rows = hidden.shape[0]
    tokens = rows // members
    depth, cols = weight.shape
    half = cols // 2
    ylo = lax.axis_index("ylo")
    z = lax.axis_index("z")
    core = lax.axis_index("core")
    low = ylo == 0

    def own(a):
        return jnp.where(low, a[:, :half], a[:, half:])

    def other(a):
        return jnp.where(low, a[:, half:], a[:, :half])

    def order(a, b, axis=0):
        return jnp.where(
            low, jnp.concatenate([a, b], axis=axis), jnp.concatenate([b, a], axis=axis)
        )

    mine, sent = own(right_factors), other(right_factors)
    slab_recv = lax.ppermute(
        jnp.concatenate([other(weight), sent, mine], axis=0), "ylo", SWAP
    )
    theirs = slab_recv[depth : depth + members]
    packed = jnp.concatenate(
        [order(own(weight), slab_recv[:depth]), order(mine, theirs)], axis=0
    )
    gathered = lax.all_gather(packed, ("z", "core"), axis=0, tiled=False)

    _, hidden_b, left_b, target_b, sent, slab_b, mine_b = lax.optimization_barrier(
        (packed, hidden, left_factors, target, sent, slab_recv, mine)
    )
    theirs_far = slab_b[depth + members :]
    right_local = jnp.concatenate([mine_b, slab_b[depth : depth + members]], axis=0)
    rows_recv = lax.ppermute(hidden_b, "ylo", SWAP)
    target_recv = lax.ppermute(other(target_b), "ylo", SWAP)
    projected_own = (
        jnp.einsum(
            "mtd,md->mt",
            hidden_b.reshape(members, tokens, features),
            left_b,
            preferred_element_type=jnp.float32,
        ).reshape(rows, 1)
        * (noise_scale / math.sqrt(features))
    )
    projected_recv = lax.ppermute(projected_own, "ylo", SWAP)
    projected = jnp.concatenate([projected_own, projected_recv], axis=0)
    target_all = jnp.concatenate([own(target_b), target_recv], axis=0)
    hidden_all = jnp.concatenate([hidden_b, rows_recv], axis=0)
    spread_rows = hidden_all.reshape(2 * rows, 2, features // (2 * depth), depth)
    hidden_all = spread_rows.transpose(0, 2, 1, 3).reshape(2 * rows, features)

    left_split = left_b.reshape(members, features // depth, depth).transpose(1, 0, 2)
    left_all = lax.all_to_all(left_split, ("ylo", "z", "core"), 0, 0, tiled=True)
    left_all = left_all.reshape(2, features // (2 * depth), members, depth)
    left_all = left_all.transpose(1, 0, 2, 3).reshape(-1, depth)
    far = order(sent, theirs_far)
    right_other = lax.all_gather(far, ("z", "core"), axis=0, tiled=False)

    hidden_all, left_all, right_other = lax.optimization_barrier((hidden_all, left_all, right_other))
    place = jnp.stack([ylo, z * 4 * members + core * 2 * members + ylo * members]).astype(jnp.int32)
    keep, send, part = project(
        place, gathered, hidden_all, target_all, right_local, projected, 32
    )

    near = lax.all_to_all(part, ("ylo", "core", "x", "yhi"), 0, 0, tiled=True)
    near = near.reshape(2, 2, 8, 2 * members).sum(axis=(0, 2)).reshape(1, 1, 4 * members)
    wide = jnp.broadcast_to(near, (16, 1, 4 * members))
    recv = lax.ppermute(send, "ylo", SWAP)
    reward = lax.all_to_all(wide, "z", 0, 0, tiled=True)

    step, fitness = step_product(place, reward, left_all, gathered, right_other, members)
    up_out = order(keep, recv, axis=1)
    return (up_out, step, fitness.reshape(members))


def solution(mesh):
    fine = Mesh(mesh.devices.reshape(SIZES), AXES)
    pop = ("ylo", "z", "core")
    shard = ("x", "yhi")
    in_specs = (P(pop, None), P(pop, shard), P(pop, None), P(pop, shard), P(pop, shard))
    out_specs = (P(pop, shard), P(pop, shard), P(pop))
    return jax.shard_map(local, mesh=fine, in_specs=in_specs, out_specs=out_specs, check_vma=False)
```

```python
import math

import jax
import jax.numpy as jnp
from jax import lax
from jax.experimental import pallas as pl
from jax.experimental.pallas import tpu as pltpu
from jax.sharding import Mesh, PartitionSpec as P

noise_scale = 0.5
spread_eps = 1e-05
AXES = ("ylo", "z", "core", "x", "yhi")
SIZES = (2, 16, 2, 4, 2)
SWAP = [(0, 1), (1, 0)]


def project_kernel(
    place, gathered, hidden_hbm, target_hbm, right, projected, keep, send, reward, total, held, hidden, target, sems
):
    chunks, slabs, width, cols = held.shape
    rows = hidden.shape[0]
    members = right.shape[0]
    tokens = rows // members
    load_hidden = pltpu.make_async_copy(hidden_hbm, hidden, sems.at[0])
    load_hidden.start()
    copies = []
    for i in range(chunks):
        copy = pltpu.make_async_copy(
            gathered.at[pl.ds(i * slabs, slabs), pl.ds(0, width), :], held.at[i], sems.at[2 + i]
        )
        copy.start()
        copies.append(copy)
    load_target = pltpu.make_async_copy(target_hbm, target, sems.at[1])
    load_target.start()
    span = slabs * width
    load_hidden.wait()
    for i in range(chunks):
        copies[i].wait()
        part = jnp.dot(
            hidden[:, i * span : (i + 1) * span],
            held[i].reshape(span, cols),
            preferred_element_type=jnp.float32,
        )
        if i == 0:
            total[...] = part
        else:
            total[...] += part
    load_target.wait()
    scale = projected[...].reshape(members, tokens, 1)
    summed = jnp.zeros((members, 1), jnp.float32)
    for at in range(0, cols, 128):
        base = total[:, at : at + 128].reshape(members, tokens, 128)
        factor = right[:, at : at + 128].astype(jnp.float32)
        value = base + scale * factor[:, None, :]
        up = value.reshape(rows, 128).astype(jnp.bfloat16)
        keep[:, at : at + 128] = up[: rows // 2]
        send[:, at : at + 128] = up[rows // 2 :]
        aim = target[:, at : at + 128].astype(jnp.float32).reshape(members, tokens, 128)
        gain = value * (0.5 + 0.5 * jnp.tanh(0.5 * value)) * aim
        summed += jnp.sum(jnp.sum(gain, axis=1), axis=-1, keepdims=True)
    shape = (members, reward.shape[-1])
    row = lax.broadcasted_iota(jnp.int32, shape, 0) + place[0] * (members // 2)
    row = jnp.where(row < members, row, row - members)
    spot = row == lax.broadcasted_iota(jnp.int32, shape, 1)
    line = jnp.sum(jnp.where(spot, summed, 0.0), axis=0, keepdims=True)
    reward[...] = jnp.broadcast_to(line[None], reward.shape)


VMEM = pl.BlockSpec(memory_space=pltpu.VMEM)
SMEM = pl.BlockSpec(memory_space=pltpu.SMEM)
ANY = pl.BlockSpec(memory_space=pl.ANY)


def project(place, gathered, hidden, target, right, projected, peers):
    blocks, _, cols = gathered.shape
    rows, features = hidden.shape
    members = right.shape[0]
    width = features // blocks
    slabs = blocks // 8
    return pl.pallas_call(
        project_kernel,
        in_specs=[SMEM, ANY, ANY, ANY, VMEM, VMEM],
        out_specs=[VMEM, VMEM, VMEM],
        out_shape=[
            jax.ShapeDtypeStruct((rows // 2, cols), jnp.bfloat16),
            jax.ShapeDtypeStruct((rows // 2, cols), jnp.bfloat16),
            jax.ShapeDtypeStruct((peers, 1, members), jnp.float32),
        ],
        scratch_shapes=[
            pltpu.VMEM((rows, cols), jnp.float32),
            pltpu.VMEM((blocks // slabs, slabs, width, cols), jnp.bfloat16),
            pltpu.VMEM(hidden.shape, jnp.bfloat16),
            pltpu.VMEM(target.shape, jnp.bfloat16),
            pltpu.SemaphoreType.DMA((blocks // slabs + 2,)),
        ],
        compiler_params=pltpu.CompilerParams(vmem_limit_bytes=53 * 1024 * 1024),
        cost_estimate=pl.CostEstimate(
            flops=2 * rows * features * cols,
            bytes_accessed=features * cols * 2,
            transcendentals=rows * cols,
        ),
    )(place, gathered, hidden, target, right, projected)


def step_kernel(place, reward, left, right_own, right_other, out, fitness):
    members, depth = left.shape
    blocks, _, lanes = reward.shape
    half = right_own.shape[2]
    own_at = pl.multiple_of(place[0] * half, 128)
    other_at = pl.multiple_of((1 - place[0]) * half, 128)
    value = reward[...].reshape(blocks, lanes)
    total = jnp.sum(jnp.sum(value, axis=0, keepdims=True), axis=1, keepdims=True)
    centered = value - total * (1.0 / members)
    squares = jnp.sum(jnp.sum(centered * centered, axis=0, keepdims=True), axis=1, keepdims=True)
    score = centered / jnp.sqrt(squares * (1.0 / members) + spread_eps)
    shape = (blocks, lanes, lanes)
    spot = lax.broadcasted_iota(jnp.int32, shape, 1) == lax.broadcasted_iota(jnp.int32, shape, 2)
    column = jnp.sum(jnp.where(spot, score[:, None, :], 0.0), axis=-1, keepdims=True)
    column = column.reshape(members, 1)
    pick = (members, fitness.shape[1])
    mine = lax.broadcasted_iota(jnp.int32, pick, 0) == (
        lax.broadcasted_iota(jnp.int32, pick, 1) + place[1]
    )
    fitness[...] = jnp.sum(jnp.where(mine, column, 0.0), axis=0, keepdims=True)
    weighted = left[...].astype(jnp.float32) * column
    high = weighted.astype(jnp.bfloat16)
    low = (weighted - high.astype(jnp.float32)).astype(jnp.bfloat16)
    both = jnp.concatenate([high, low], axis=1)

    def multiply(right, at):
        product = lax.dot_general(
            both,
            right.reshape(members, half),
            (((0,), (0,)), ((), ())),
            preferred_element_type=jnp.float32,
        )
        out[:, pl.ds(at, half)] = (product[:depth] + product[depth:]) * (1.0 / math.sqrt(members))

    multiply(right_other[...], other_at)
    multiply(right_own[...], own_at)


def step_product(place, reward, left, right_own, right_other, own):
    members, depth = left.shape
    half = right_other.shape[2]
    return pl.pallas_call(
        step_kernel,
        in_specs=[SMEM, VMEM, VMEM, VMEM, VMEM],
        out_specs=[VMEM, VMEM],
        out_shape=[
            jax.ShapeDtypeStruct((depth, 2 * half), jnp.float32),
            jax.ShapeDtypeStruct((1, own), jnp.float32),
        ],
        compiler_params=pltpu.CompilerParams(vmem_limit_bytes=24 * 1024 * 1024),
        cost_estimate=pl.CostEstimate(
            flops=128 * depth * members * half,
            bytes_accessed=members * half * 4 + depth * half * 8,
            transcendentals=0,
        ),
    )(place, reward, left, right_own, right_other)


def local(hidden, weight, left_factors, right_factors, target):
    members, features = left_factors.shape
    rows = hidden.shape[0]
    tokens = rows // members
    depth, cols = weight.shape
    half = cols // 2
    ylo = lax.axis_index("ylo")
    z = lax.axis_index("z")
    core = lax.axis_index("core")
    low = ylo == 0

    def own(a):
        return jnp.where(low, a[:, :half], a[:, half:])

    def other(a):
        return jnp.where(low, a[:, half:], a[:, :half])

    def order(a, b, axis=0):
        return jnp.where(
            low, jnp.concatenate([a, b], axis=axis), jnp.concatenate([b, a], axis=axis)
        )

    mine, sent = own(right_factors), other(right_factors)
    slab_recv = lax.ppermute(
        jnp.concatenate([other(weight), sent, mine], axis=0), "ylo", SWAP
    )
    theirs = slab_recv[depth : depth + members]
    packed = jnp.concatenate(
        [order(own(weight), slab_recv[:depth]), order(mine, theirs)], axis=0
    )
    gathered = lax.all_gather(packed, ("z", "core"), axis=0, tiled=False)

    _, hidden_b, left_b, target_b, sent, slab_b, mine_b = lax.optimization_barrier(
        (packed, hidden, left_factors, target, sent, slab_recv, mine)
    )
    theirs_far = slab_b[depth + members :]
    right_local = jnp.concatenate([mine_b, slab_b[depth : depth + members]], axis=0)
    rows_recv = lax.ppermute(hidden_b, "ylo", SWAP)
    target_recv = lax.ppermute(other(target_b), "ylo", SWAP)
    projected_own = (
        jnp.einsum(
            "mtd,md->mt",
            hidden_b.reshape(members, tokens, features),
            left_b,
            preferred_element_type=jnp.float32,
        ).reshape(rows, 1)
        * (noise_scale / math.sqrt(features))
    )
    projected_recv = lax.ppermute(projected_own, "ylo", SWAP)
    projected = jnp.concatenate([projected_own, projected_recv], axis=0)
    target_all = jnp.concatenate([own(target_b), target_recv], axis=0)
    hidden_all = jnp.concatenate([hidden_b, rows_recv], axis=0)
    spread_rows = hidden_all.reshape(2 * rows, 2, features // (2 * depth), depth)
    hidden_all = spread_rows.transpose(0, 2, 1, 3).reshape(2 * rows, features)

    left_split = left_b.reshape(members, features // depth, depth).transpose(1, 0, 2)
    left_all = lax.all_to_all(left_split, ("ylo", "z", "core"), 0, 0, tiled=True)
    left_all = left_all.reshape(2, features // (2 * depth), members, depth)
    left_all = left_all.transpose(1, 0, 2, 3).reshape(-1, depth)
    far = order(sent, theirs_far)
    right_other = lax.all_gather(far, ("z", "core"), axis=0, tiled=False)

    hidden_all, left_all, right_other = lax.optimization_barrier((hidden_all, left_all, right_other))
    place = jnp.stack([ylo, z * 4 * members + core * 2 * members + ylo * members]).astype(jnp.int32)
    keep, send, part = project(
        place, gathered, hidden_all, target_all, right_local, projected, 32
    )

    gathered, part = lax.optimization_barrier((gathered, part))
    right_own = gathered[:, 2 * depth :]
    near = lax.all_to_all(part, ("ylo", "core", "x", "yhi"), 0, 0, tiled=True)
    near = near.reshape(2, 2, 8, 2 * members).sum(axis=(0, 2)).reshape(1, 1, 4 * members)
    reward = lax.all_to_all(jnp.broadcast_to(near, (16, 1, 4 * members)), "z", 0, 0, tiled=True)
    recv = lax.ppermute(send, "ylo", SWAP)
    up_out = order(keep, recv, axis=1)
    step, fitness = step_product(place, reward, left_all, right_own, right_other, members)
    return (up_out, step, fitness.reshape(members))


def solution(mesh):
    fine = Mesh(mesh.devices.reshape(SIZES), AXES)
    pop = ("ylo", "z", "core")
    shard = ("x", "yhi")
    in_specs = (P(pop, None), P(pop, shard), P(pop, None), P(pop, shard), P(pop, shard))
    out_specs = (P(pop, shard), P(pop, shard), P(pop))
    return jax.shard_map(local, mesh=fine, in_specs=in_specs, out_specs=out_specs, check_vma=False)
```

```python
import math

import jax
import jax.numpy as jnp
from jax import lax
from jax.experimental import pallas as pl
from jax.experimental.pallas import tpu as pltpu
from jax.sharding import Mesh, PartitionSpec as P

noise_scale = 0.5
spread_eps = 1e-05
AXES = ("ylo", "z", "core", "x", "yhi")
SIZES = (2, 16, 2, 4, 2)
SWAP = [(0, 1), (1, 0)]


def project_kernel(
    place, gathered, hidden_hbm, target_hbm, right, projected, keep, send, reward, total, held, hidden, target, sems
):
    chunks, slabs, width, cols = held.shape
    rows = hidden.shape[0]
    members = right.shape[0]
    tokens = rows // members
    load_hidden = pltpu.make_async_copy(hidden_hbm, hidden, sems.at[0])
    load_hidden.start()
    copies = []
    for i in range(chunks):
        copy = pltpu.make_async_copy(
            gathered.at[pl.ds(i * slabs, slabs), pl.ds(0, width), :], held.at[i], sems.at[2 + i]
        )
        copy.start()
        copies.append(copy)
    load_target = pltpu.make_async_copy(target_hbm, target, sems.at[1])
    load_target.start()
    span = slabs * width
    load_hidden.wait()
    for i in range(chunks):
        copies[i].wait()
        part = jnp.dot(
            hidden[:, i * span : (i + 1) * span],
            held[i].reshape(span, cols),
            preferred_element_type=jnp.float32,
        )
        if i == 0:
            total[...] = part
        else:
            total[...] += part
    load_target.wait()
    scale = projected[...].reshape(members, tokens, 1)
    summed = jnp.zeros((members, 1), jnp.float32)
    for at in range(0, cols, 128):
        base = total[:, at : at + 128].reshape(members, tokens, 128)
        factor = right[:, at : at + 128].astype(jnp.float32)
        value = base + scale * factor[:, None, :]
        up = value.reshape(rows, 128).astype(jnp.bfloat16)
        keep[:, at : at + 128] = up[: rows // 2]
        send[:, at : at + 128] = up[rows // 2 :]
        aim = target[:, at : at + 128].astype(jnp.float32).reshape(members, tokens, 128)
        gain = value * (0.5 + 0.5 * jnp.tanh(0.5 * value)) * aim
        summed += jnp.sum(jnp.sum(gain, axis=1), axis=-1, keepdims=True)
    shape = (members, reward.shape[-1])
    row = lax.broadcasted_iota(jnp.int32, shape, 0) + place[0] * (members // 2)
    row = jnp.where(row < members, row, row - members)
    spot = row == lax.broadcasted_iota(jnp.int32, shape, 1)
    line = jnp.sum(jnp.where(spot, summed, 0.0), axis=0, keepdims=True)
    reward[...] = jnp.broadcast_to(line[None], reward.shape)


VMEM = pl.BlockSpec(memory_space=pltpu.VMEM)
SMEM = pl.BlockSpec(memory_space=pltpu.SMEM)
ANY = pl.BlockSpec(memory_space=pl.ANY)


def project(place, gathered, hidden, target, right, projected, peers):
    blocks, _, cols = gathered.shape
    rows, features = hidden.shape
    members = right.shape[0]
    width = features // blocks
    slabs = blocks // 8
    return pl.pallas_call(
        project_kernel,
        in_specs=[SMEM, ANY, ANY, ANY, VMEM, VMEM],
        out_specs=[VMEM, VMEM, VMEM],
        out_shape=[
            jax.ShapeDtypeStruct((rows // 2, cols), jnp.bfloat16),
            jax.ShapeDtypeStruct((rows // 2, cols), jnp.bfloat16),
            jax.ShapeDtypeStruct((peers, 1, members), jnp.float32),
        ],
        scratch_shapes=[
            pltpu.VMEM((rows, cols), jnp.float32),
            pltpu.VMEM((blocks // slabs, slabs, width, cols), jnp.bfloat16),
            pltpu.VMEM(hidden.shape, jnp.bfloat16),
            pltpu.VMEM(target.shape, jnp.bfloat16),
            pltpu.SemaphoreType.DMA((blocks // slabs + 2,)),
        ],
        compiler_params=pltpu.CompilerParams(vmem_limit_bytes=53 * 1024 * 1024),
        cost_estimate=pl.CostEstimate(
            flops=2 * rows * features * cols,
            bytes_accessed=features * cols * 2,
            transcendentals=rows * cols,
        ),
    )(place, gathered, hidden, target, right, projected)


def step_kernel(place, reward, left, right_left, right_right, out, fitness):
    members, depth = left.shape
    blocks, _, lanes = reward.shape
    half = right_left.shape[2]
    value = reward[...].reshape(blocks, lanes)
    total = jnp.sum(jnp.sum(value, axis=0, keepdims=True), axis=1, keepdims=True)
    centered = value - total * (1.0 / members)
    squares = jnp.sum(jnp.sum(centered * centered, axis=0, keepdims=True), axis=1, keepdims=True)
    score = centered / jnp.sqrt(squares * (1.0 / members) + spread_eps)
    shape = (blocks, lanes, lanes)
    spot = lax.broadcasted_iota(jnp.int32, shape, 1) == lax.broadcasted_iota(jnp.int32, shape, 2)
    column = jnp.sum(jnp.where(spot, score[:, None, :], 0.0), axis=-1, keepdims=True)
    column = column.reshape(members, 1)
    pick = (members, fitness.shape[1])
    mine = lax.broadcasted_iota(jnp.int32, pick, 0) == (
        lax.broadcasted_iota(jnp.int32, pick, 1) + place[1]
    )
    fitness[...] = jnp.sum(jnp.where(mine, column, 0.0), axis=0, keepdims=True)
    weighted = left[...].astype(jnp.float32) * column
    high = weighted.astype(jnp.bfloat16)
    low = (weighted - high.astype(jnp.float32)).astype(jnp.bfloat16)
    both = jnp.concatenate([high, low], axis=1)

    def multiply(right, at):
        product = lax.dot_general(
            both,
            right.reshape(members, half),
            (((0,), (0,)), ((), ())),
            preferred_element_type=jnp.float32,
        )
        out[:, at : at + half] = (product[:depth] + product[depth:]) * (1.0 / math.sqrt(members))

    multiply(right_left[...], 0)
    multiply(right_right[...], half)


def step_product(place, reward, left, right_left, right_right, own):
    members, depth = left.shape
    half = right_right.shape[2]
    return pl.pallas_call(
        step_kernel,
        in_specs=[SMEM, VMEM, VMEM, VMEM, VMEM],
        out_specs=[VMEM, VMEM],
        out_shape=[
            jax.ShapeDtypeStruct((depth, 2 * half), jnp.float32),
            jax.ShapeDtypeStruct((1, own), jnp.float32),
        ],
        compiler_params=pltpu.CompilerParams(vmem_limit_bytes=24 * 1024 * 1024),
        cost_estimate=pl.CostEstimate(
            flops=128 * depth * members * half,
            bytes_accessed=members * half * 4 + depth * half * 8,
            transcendentals=0,
        ),
    )(place, reward, left, right_left, right_right)


def local(hidden, weight, left_factors, right_factors, target):
    members, features = left_factors.shape
    rows = hidden.shape[0]
    tokens = rows // members
    depth, cols = weight.shape
    half = cols // 2
    ylo = lax.axis_index("ylo")
    z = lax.axis_index("z")
    core = lax.axis_index("core")
    low = ylo == 0

    def own(a):
        return jnp.where(low, a[:, :half], a[:, half:])

    def other(a):
        return jnp.where(low, a[:, half:], a[:, :half])

    def order(a, b, axis=0):
        return jnp.where(
            low, jnp.concatenate([a, b], axis=axis), jnp.concatenate([b, a], axis=axis)
        )

    near_left, near_right = right_factors[:, :half], right_factors[:, half:]
    slab_recv = lax.ppermute(
        jnp.concatenate([other(weight), near_left, near_right], axis=0), "ylo", SWAP
    )
    packed = jnp.concatenate(
        [
            order(own(weight), slab_recv[:depth]),
            order(near_left, slab_recv[depth : depth + members]),
            order(near_right, slab_recv[depth + members :]),
        ],
        axis=0,
    )
    gathered = lax.all_gather(packed, ("z", "core"), axis=0, tiled=False)

    _, hidden_b, left_b, target_b, right_b, slab_b = lax.optimization_barrier(
        (packed, hidden, left_factors, target, right_factors, slab_recv)
    )
    theirs = jnp.where(low, slab_b[depth : depth + members], slab_b[depth + members :])
    right_local = jnp.concatenate([own(right_b), theirs], axis=0)
    rows_recv = lax.ppermute(hidden_b, "ylo", SWAP)
    target_recv = lax.ppermute(other(target_b), "ylo", SWAP)
    projected_own = (
        jnp.einsum(
            "mtd,md->mt",
            hidden_b.reshape(members, tokens, features),
            left_b,
            preferred_element_type=jnp.float32,
        ).reshape(rows, 1)
        * (noise_scale / math.sqrt(features))
    )
    projected_recv = lax.ppermute(projected_own, "ylo", SWAP)
    projected = jnp.concatenate([projected_own, projected_recv], axis=0)
    target_all = jnp.concatenate([own(target_b), target_recv], axis=0)
    hidden_all = jnp.concatenate([hidden_b, rows_recv], axis=0)
    spread_rows = hidden_all.reshape(2 * rows, 2, features // (2 * depth), depth)
    hidden_all = spread_rows.transpose(0, 2, 1, 3).reshape(2 * rows, features)

    left_split = left_b.reshape(members, features // depth, depth).transpose(1, 0, 2)
    left_all = lax.all_to_all(left_split, ("ylo", "z", "core"), 0, 0, tiled=True)
    left_all = left_all.reshape(2, features // (2 * depth), members, depth)
    left_all = left_all.transpose(1, 0, 2, 3).reshape(-1, depth)
    hidden_all, left_all = lax.optimization_barrier((hidden_all, left_all))
    place = jnp.stack([ylo, z * 4 * members + core * 2 * members + ylo * members]).astype(jnp.int32)
    keep, send, part = project(
        place, gathered, hidden_all, target_all, right_local, projected, 32
    )

    gathered, part = lax.optimization_barrier((gathered, part))
    right_left = gathered[:, 2 * depth : 2 * depth + 2 * members]
    right_right = gathered[:, 2 * depth + 2 * members :]
    near = lax.all_to_all(part, ("ylo", "core", "x", "yhi"), 0, 0, tiled=True)
    near = near.reshape(2, 2, 8, 2 * members).sum(axis=(0, 2)).reshape(1, 1, 4 * members)
    reward = lax.all_to_all(jnp.broadcast_to(near, (16, 1, 4 * members)), "z", 0, 0, tiled=True)
    recv = lax.ppermute(send, "ylo", SWAP)
    up_out = order(keep, recv, axis=1)
    step, fitness = step_product(place, reward, left_all, right_left, right_right, members)
    return (up_out, step, fitness.reshape(members))


def solution(mesh):
    fine = Mesh(mesh.devices.reshape(SIZES), AXES)
    pop = ("ylo", "z", "core")
    shard = ("x", "yhi")
    in_specs = (P(pop, None), P(pop, shard), P(pop, None), P(pop, shard), P(pop, shard))
    out_specs = (P(pop, shard), P(pop, shard), P(pop))
    return jax.shard_map(local, mesh=fine, in_specs=in_specs, out_specs=out_specs, check_vma=False)
```

```python
import math

import jax
import jax.numpy as jnp
from jax import lax
from jax.experimental import pallas as pl
from jax.experimental.pallas import tpu as pltpu
from jax.sharding import Mesh, PartitionSpec as P

noise_scale = 0.5
spread_eps = 1e-05
AXES = ("ylo", "z", "core", "x", "yhi")
SIZES = (2, 16, 2, 4, 2)
SWAP = [(0, 1), (1, 0)]


def project_kernel(
    place, gathered, hidden_hbm, target_hbm, right, projected, keep, send, reward, total, held, hidden, target, sems
):
    chunks, slabs, width, cols = held.shape
    rows = hidden.shape[0]
    members = right.shape[0]
    tokens = rows // members
    load_hidden = pltpu.make_async_copy(hidden_hbm, hidden, sems.at[0])
    load_hidden.start()
    copies = []
    deep = width // 2
    for i in range(chunks):
        for j in range(2):
            copy = pltpu.make_async_copy(
                gathered.at[pl.ds(i * slabs, slabs), pl.ds(0, deep), pl.ds(j * cols, cols)],
                held.at[i, :, pl.ds(j * deep, deep), :],
                sems.at[2 + 2 * i + j],
            )
            copy.start()
            copies.append(copy)
    load_target = pltpu.make_async_copy(target_hbm, target, sems.at[1])
    load_target.start()
    span = slabs * width
    load_hidden.wait()
    for i in range(chunks):
        copies[2 * i].wait()
        copies[2 * i + 1].wait()
        part = jnp.dot(
            hidden[:, i * span : (i + 1) * span],
            held[i].reshape(span, cols),
            preferred_element_type=jnp.float32,
        )
        if i == 0:
            total[...] = part
        else:
            total[...] += part
    load_target.wait()
    scale = projected[...].reshape(members, tokens, 1)
    summed = jnp.zeros((members, 1), jnp.float32)
    for at in range(0, cols, 128):
        base = total[:, at : at + 128].reshape(members, tokens, 128)
        factor = right[:, at : at + 128].astype(jnp.float32)
        value = base + scale * factor[:, None, :]
        up = value.reshape(rows, 128).astype(jnp.bfloat16)
        keep[:, at : at + 128] = up[: rows // 2]
        send[:, at : at + 128] = up[rows // 2 :]
        aim = target[:, at : at + 128].astype(jnp.float32).reshape(members, tokens, 128)
        gain = value * (0.5 + 0.5 * jnp.tanh(0.5 * value)) * aim
        summed += jnp.sum(jnp.sum(gain, axis=1), axis=-1, keepdims=True)
    shape = (members, reward.shape[-1])
    row = lax.broadcasted_iota(jnp.int32, shape, 0) + place[0] * (members // 2)
    row = jnp.where(row < members, row, row - members)
    spot = row == lax.broadcasted_iota(jnp.int32, shape, 1)
    line = jnp.sum(jnp.where(spot, summed, 0.0), axis=0, keepdims=True)
    reward[...] = jnp.broadcast_to(line[None], reward.shape)


VMEM = pl.BlockSpec(memory_space=pltpu.VMEM)
SMEM = pl.BlockSpec(memory_space=pltpu.SMEM)
ANY = pl.BlockSpec(memory_space=pl.ANY)


def project(place, gathered, hidden, target, right, projected, peers):
    blocks = gathered.shape[0]
    cols = target.shape[1]
    rows, features = hidden.shape
    members = right.shape[0]
    width = features // blocks
    slabs = blocks // 8
    return pl.pallas_call(
        project_kernel,
        in_specs=[SMEM, ANY, ANY, ANY, VMEM, VMEM],
        out_specs=[VMEM, VMEM, VMEM],
        out_shape=[
            jax.ShapeDtypeStruct((rows // 2, cols), jnp.bfloat16),
            jax.ShapeDtypeStruct((rows // 2, cols), jnp.bfloat16),
            jax.ShapeDtypeStruct((peers, 1, members), jnp.float32),
        ],
        scratch_shapes=[
            pltpu.VMEM((rows, cols), jnp.float32),
            pltpu.VMEM((blocks // slabs, slabs, width, cols), jnp.bfloat16),
            pltpu.VMEM(hidden.shape, jnp.bfloat16),
            pltpu.VMEM(target.shape, jnp.bfloat16),
            pltpu.SemaphoreType.DMA((2 * (blocks // slabs) + 2,)),
        ],
        compiler_params=pltpu.CompilerParams(vmem_limit_bytes=53 * 1024 * 1024),
        cost_estimate=pl.CostEstimate(
            flops=2 * rows * features * cols,
            bytes_accessed=features * cols * 2,
            transcendentals=rows * cols,
        ),
    )(place, gathered, hidden, target, right, projected)


def step_kernel(place, reward, left, right, out, fitness):
    members, depth = left.shape
    blocks, _, lanes = reward.shape
    cols = right.shape[2]
    value = reward[...].reshape(blocks, lanes)
    total = jnp.sum(jnp.sum(value, axis=0, keepdims=True), axis=1, keepdims=True)
    centered = value - total * (1.0 / members)
    squares = jnp.sum(jnp.sum(centered * centered, axis=0, keepdims=True), axis=1, keepdims=True)
    score = centered / jnp.sqrt(squares * (1.0 / members) + spread_eps)
    shape = (blocks, lanes, lanes)
    spot = lax.broadcasted_iota(jnp.int32, shape, 1) == lax.broadcasted_iota(jnp.int32, shape, 2)
    column = jnp.sum(jnp.where(spot, score[:, None, :], 0.0), axis=-1, keepdims=True)
    column = column.reshape(members, 1)
    pick = (members, fitness.shape[1])
    mine = lax.broadcasted_iota(jnp.int32, pick, 0) == (
        lax.broadcasted_iota(jnp.int32, pick, 1) + place[1]
    )
    fitness[...] = jnp.sum(jnp.where(mine, column, 0.0), axis=0, keepdims=True)
    weighted = left[...].astype(jnp.float32) * column
    high = weighted.astype(jnp.bfloat16)
    low = (weighted - high.astype(jnp.float32)).astype(jnp.bfloat16)
    both = jnp.concatenate([high, low], axis=1)

    factors = right[...].reshape(members, cols)
    for at in range(0, cols, cols // 2):
        product = lax.dot_general(
            both,
            factors[:, at : at + cols // 2],
            (((0,), (0,)), ((), ())),
            preferred_element_type=jnp.float32,
        )
        out[:, at : at + cols // 2] = (product[:depth] + product[depth:]) * (
            1.0 / math.sqrt(members)
        )


def step_product(place, reward, left, right, own):
    members, depth = left.shape
    cols = right.shape[2]
    return pl.pallas_call(
        step_kernel,
        in_specs=[SMEM, VMEM, VMEM, VMEM],
        out_specs=[VMEM, VMEM],
        out_shape=[
            jax.ShapeDtypeStruct((depth, cols), jnp.float32),
            jax.ShapeDtypeStruct((1, own), jnp.float32),
        ],
        compiler_params=pltpu.CompilerParams(vmem_limit_bytes=24 * 1024 * 1024),
        cost_estimate=pl.CostEstimate(
            flops=128 * depth * members * cols,
            bytes_accessed=members * cols * 4 + depth * cols * 4,
            transcendentals=0,
        ),
    )(place, reward, left, right)


def local(hidden, weight, left_factors, right_factors, target):
    members, features = left_factors.shape
    rows = hidden.shape[0]
    tokens = rows // members
    depth, cols = weight.shape
    half = cols // 2
    ylo = lax.axis_index("ylo")
    z = lax.axis_index("z")
    core = lax.axis_index("core")
    low = ylo == 0

    def own(a):
        return jnp.where(low, a[:, :half], a[:, half:])

    def other(a):
        return jnp.where(low, a[:, half:], a[:, :half])

    def order(a, b, axis=0):
        return jnp.where(
            low, jnp.concatenate([a, b], axis=axis), jnp.concatenate([b, a], axis=axis)
        )

    far = other(weight)
    far = jnp.concatenate([far[: depth // 2], far[depth // 2 :]], axis=1)
    slab_recv = lax.ppermute(jnp.concatenate([far, right_factors], axis=0), "ylo", SWAP)
    weight_recv = slab_recv[: depth // 2]
    weight_recv = jnp.concatenate([weight_recv[:, :half], weight_recv[:, half:]], axis=0)
    packed = jnp.concatenate(
        [
            order(own(weight), weight_recv, axis=1),
            order(right_factors, slab_recv[depth // 2 :]),
        ],
        axis=0,
    )
    gathered = lax.all_gather(packed, ("z", "core"), axis=0, tiled=False)

    _, hidden_b, left_b, target_b, right_b, slab_b = lax.optimization_barrier(
        (packed, hidden, left_factors, target, right_factors, slab_recv)
    )
    right_local = jnp.concatenate([own(right_b), own(slab_b[depth // 2 :])], axis=0)
    rows_recv = lax.ppermute(hidden_b, "ylo", SWAP)
    target_recv = lax.ppermute(other(target_b), "ylo", SWAP)
    projected_own = (
        jnp.einsum(
            "mtd,md->mt",
            hidden_b.reshape(members, tokens, features),
            left_b,
            preferred_element_type=jnp.float32,
        ).reshape(rows, 1)
        * (noise_scale / math.sqrt(features))
    )
    projected_recv = lax.ppermute(projected_own, "ylo", SWAP)
    projected = jnp.concatenate([projected_own, projected_recv], axis=0)
    target_all = jnp.concatenate([own(target_b), target_recv], axis=0)
    hidden_all = jnp.concatenate([hidden_b, rows_recv], axis=0)
    spread_rows = hidden_all.reshape(2 * rows, 2, features // (2 * depth), depth)
    hidden_all = spread_rows.transpose(0, 2, 1, 3).reshape(2 * rows, features)

    left_split = left_b.reshape(members, features // depth, depth).transpose(1, 0, 2)
    left_all = lax.all_to_all(left_split, ("ylo", "z", "core"), 0, 0, tiled=True)
    left_all = left_all.reshape(2, features // (2 * depth), members, depth)
    left_all = left_all.transpose(1, 0, 2, 3).reshape(-1, depth)
    hidden_all, left_all = lax.optimization_barrier((hidden_all, left_all))
    place = jnp.stack([ylo, z * 4 * members + core * 2 * members + ylo * members]).astype(jnp.int32)
    keep, send, part = project(
        place, gathered, hidden_all, target_all, right_local, projected, 32
    )

    gathered, part = lax.optimization_barrier((gathered, part))
    right_all = gathered[:, depth:]
    near = lax.all_to_all(part, ("ylo", "core", "x", "yhi"), 0, 0, tiled=True)
    near = near.reshape(2, 2, 8, 2 * members).sum(axis=(0, 2)).reshape(1, 1, 4 * members)
    reward = lax.all_to_all(jnp.broadcast_to(near, (16, 1, 4 * members)), "z", 0, 0, tiled=True)
    recv = lax.ppermute(send, "ylo", SWAP)
    up_out = order(keep, recv, axis=1)
    step, fitness = step_product(place, reward, left_all, right_all, members)
    return (up_out, step, fitness.reshape(members))


def solution(mesh):
    fine = Mesh(mesh.devices.reshape(SIZES), AXES)
    pop = ("ylo", "z", "core")
    shard = ("x", "yhi")
    in_specs = (P(pop, None), P(pop, shard), P(pop, None), P(pop, shard), P(pop, shard))
    out_specs = (P(pop, shard), P(pop, shard), P(pop))
    return jax.shard_map(local, mesh=fine, in_specs=in_specs, out_specs=out_specs, check_vma=False)
```

```python
import math

import jax
import jax.numpy as jnp
from jax import lax
from jax.experimental import pallas as pl
from jax.experimental.pallas import tpu as pltpu
from jax.sharding import Mesh, PartitionSpec as P

noise_scale = 0.5
spread_eps = 1e-05
AXES = ("ylo", "z", "core", "x", "yhi")
SIZES = (2, 16, 2, 4, 2)
SWAP = [(0, 1), (1, 0)]


def project_kernel(
    place, gathered, hidden_hbm, target_hbm, right, projected, keep, send, reward, total, held, hidden, target, sems
):
    chunks, slabs, width, cols = held.shape
    rows = hidden.shape[0]
    members = right.shape[0]
    tokens = rows // members
    load_hidden = pltpu.make_async_copy(hidden_hbm, hidden, sems.at[0])
    load_hidden.start()
    copies = []
    for i in range(chunks):
        copy = pltpu.make_async_copy(
            gathered.at[pl.ds(i * slabs, slabs), pl.ds(0, width), :], held.at[i], sems.at[2 + i]
        )
        copy.start()
        copies.append(copy)
    load_target = pltpu.make_async_copy(target_hbm, target, sems.at[1])
    load_target.start()
    span = slabs * width
    load_hidden.wait()
    for i in range(chunks):
        copies[i].wait()
        part = jnp.dot(
            hidden[:, i * span : (i + 1) * span],
            held[i].reshape(span, cols),
            preferred_element_type=jnp.float32,
        )
        if i == 0:
            total[...] = part
        else:
            total[...] += part
    load_target.wait()
    scale = projected[...].reshape(members, tokens, 1)
    summed = jnp.zeros((members, 1), jnp.float32)
    for at in range(0, cols, 128):
        base = total[:, at : at + 128].reshape(members, tokens, 128)
        factor = right[:, at : at + 128].astype(jnp.float32)
        value = base + scale * factor[:, None, :]
        up = value.reshape(rows, 128).astype(jnp.bfloat16)
        keep[:, at : at + 128] = up[: rows // 2]
        send[:, at : at + 128] = up[rows // 2 :]
        aim = target[:, at : at + 128].astype(jnp.float32).reshape(members, tokens, 128)
        gain = value * (0.5 + 0.5 * jnp.tanh(0.5 * value)) * aim
        summed += jnp.sum(jnp.sum(gain, axis=1), axis=-1, keepdims=True)
    shape = (members, reward.shape[-1])
    row = lax.broadcasted_iota(jnp.int32, shape, 0) + place[0] * (members // 2)
    row = jnp.where(row < members, row, row - members)
    spot = row == lax.broadcasted_iota(jnp.int32, shape, 1)
    line = jnp.sum(jnp.where(spot, summed, 0.0), axis=0, keepdims=True)
    reward[...] = jnp.broadcast_to(line[None], reward.shape)


VMEM = pl.BlockSpec(memory_space=pltpu.VMEM)
SMEM = pl.BlockSpec(memory_space=pltpu.SMEM)
ANY = pl.BlockSpec(memory_space=pl.ANY)


def project(place, gathered, hidden, target, right, projected, peers):
    blocks, _, cols = gathered.shape
    rows, features = hidden.shape
    members = right.shape[0]
    width = features // blocks
    slabs = blocks // 8
    return pl.pallas_call(
        project_kernel,
        in_specs=[SMEM, ANY, ANY, ANY, VMEM, VMEM],
        out_specs=[VMEM, VMEM, VMEM],
        out_shape=[
            jax.ShapeDtypeStruct((rows // 2, cols), jnp.bfloat16),
            jax.ShapeDtypeStruct((rows // 2, cols), jnp.bfloat16),
            jax.ShapeDtypeStruct((peers, 1, members), jnp.float32),
        ],
        scratch_shapes=[
            pltpu.VMEM((rows, cols), jnp.float32),
            pltpu.VMEM((blocks // slabs, slabs, width, cols), jnp.bfloat16),
            pltpu.VMEM(hidden.shape, jnp.bfloat16),
            pltpu.VMEM(target.shape, jnp.bfloat16),
            pltpu.SemaphoreType.DMA((blocks // slabs + 2,)),
        ],
        compiler_params=pltpu.CompilerParams(vmem_limit_bytes=53 * 1024 * 1024),
        cost_estimate=pl.CostEstimate(
            flops=2 * rows * features * cols,
            bytes_accessed=features * cols * 2,
            transcendentals=rows * cols,
        ),
    )(place, gathered, hidden, target, right, projected)


def step_kernel(place, reward, left, right_own, right_other, out, fitness):
    members, depth = left.shape
    blocks, _, lanes = reward.shape
    value = reward[...].reshape(blocks, lanes)
    total = jnp.sum(jnp.sum(value, axis=0, keepdims=True), axis=1, keepdims=True)
    centered = value - total * (1.0 / members)
    squares = jnp.sum(jnp.sum(centered * centered, axis=0, keepdims=True), axis=1, keepdims=True)
    score = centered / jnp.sqrt(squares * (1.0 / members) + spread_eps)
    run = fitness.shape[1]
    shape = (blocks, lanes // 2, lanes)
    index = lax.broadcasted_iota(jnp.int32, shape, 1)
    lane = lax.broadcasted_iota(jnp.int32, shape, 2)
    columns = []
    for side in (place[0], 1 - place[0]):
        spot = lane == index + jnp.where(index < run, 0, run) + side * run
        column = jnp.sum(jnp.where(spot, score[:, None, :], 0.0), axis=-1, keepdims=True)
        columns.append(column.reshape(members // 2, 1))
    pick = (members // 2, run)
    mine = lax.broadcasted_iota(jnp.int32, pick, 0) == (
        lax.broadcasted_iota(jnp.int32, pick, 1) + place[1]
    )
    fitness[...] = jnp.sum(jnp.where(mine, columns[0], 0.0), axis=0, keepdims=True)
    both = []
    for side, column in enumerate(columns):
        rows = left[side * (members // 2) : (side + 1) * (members // 2)]
        weighted = rows.astype(jnp.float32) * column
        high = weighted.astype(jnp.bfloat16)
        low = (weighted - high.astype(jnp.float32)).astype(jnp.bfloat16)
        both.append(jnp.concatenate([high, low], axis=1))
    cols = right_own.shape[1]
    for at in range(0, cols, cols // 2):
        product = sum(
            lax.dot_general(
                factor,
                right[:, at : at + cols // 2],
                (((0,), (0,)), ((), ())),
                preferred_element_type=jnp.float32,
            )
            for factor, right in zip(both, (right_own, right_other))
        )
        out[:, at : at + cols // 2] = (product[:depth] + product[depth:]) * (
            1.0 / math.sqrt(members)
        )


def step_product(place, reward, left, right_own, right_other, own):
    members, depth = left.shape
    cols = right_own.shape[1]
    return pl.pallas_call(
        step_kernel,
        in_specs=[SMEM, VMEM, VMEM, VMEM, VMEM],
        out_specs=[VMEM, VMEM],
        out_shape=[
            jax.ShapeDtypeStruct((depth, cols), jnp.float32),
            jax.ShapeDtypeStruct((1, own), jnp.float32),
        ],
        compiler_params=pltpu.CompilerParams(vmem_limit_bytes=24 * 1024 * 1024),
        cost_estimate=pl.CostEstimate(
            flops=128 * depth * members * cols,
            bytes_accessed=members * cols * 4 + depth * cols * 4,
            transcendentals=0,
        ),
    )(place, reward, left, right_own, right_other)


def local(hidden, weight, left_factors, right_factors, target):
    members, features = left_factors.shape
    rows = hidden.shape[0]
    tokens = rows // members
    depth, cols = weight.shape
    half = cols // 2
    ylo = lax.axis_index("ylo")
    z = lax.axis_index("z")
    core = lax.axis_index("core")
    low = ylo == 0

    def own(a):
        return jnp.where(low, a[:, :half], a[:, half:])

    def other(a):
        return jnp.where(low, a[:, half:], a[:, :half])

    def order(a, b, axis=0):
        return jnp.where(
            low, jnp.concatenate([a, b], axis=axis), jnp.concatenate([b, a], axis=axis)
        )

    weight_recv = lax.ppermute(other(weight), "ylo", SWAP)
    packed = order(own(weight), weight_recv)
    gathered = lax.all_gather(packed, ("z", "core"), axis=0, tiled=False)

    _, hidden_b, left_b, target_b, right_b = lax.optimization_barrier(
        (packed, hidden, left_factors, target, right_factors)
    )
    right_own = lax.all_gather(right_b, ("z", "core"), axis=0, tiled=True)
    right_other = lax.ppermute(right_own, "ylo", SWAP)
    right_recv = lax.ppermute(other(right_b), "ylo", SWAP)
    right_local = jnp.concatenate([own(right_b), right_recv], axis=0)
    rows_recv = lax.ppermute(hidden_b, "ylo", SWAP)
    target_recv = lax.ppermute(other(target_b), "ylo", SWAP)
    projected_own = (
        jnp.einsum(
            "mtd,md->mt",
            hidden_b.reshape(members, tokens, features),
            left_b,
            preferred_element_type=jnp.float32,
        ).reshape(rows, 1)
        * (noise_scale / math.sqrt(features))
    )
    projected_recv = lax.ppermute(projected_own, "ylo", SWAP)
    projected = jnp.concatenate([projected_own, projected_recv], axis=0)
    target_all = jnp.concatenate([own(target_b), target_recv], axis=0)
    hidden_all = jnp.concatenate([hidden_b, rows_recv], axis=0)
    spread_rows = hidden_all.reshape(2 * rows, 2, features // (2 * depth), depth)
    hidden_all = spread_rows.transpose(0, 2, 1, 3).reshape(2 * rows, features)

    left_split = left_b.reshape(members, features // depth, depth).transpose(1, 0, 2)
    left_all = lax.all_to_all(left_split, ("ylo", "z", "core"), 0, 0, tiled=True)
    left_all = left_all.reshape(2, features // (2 * depth), members, depth)
    left_all = jnp.where(low, left_all, left_all[::-1]).reshape(-1, depth)
    hidden_all, left_all, right_own = lax.optimization_barrier((hidden_all, left_all, right_own))
    place = jnp.stack([ylo, z * 2 * members + core * members]).astype(jnp.int32)
    keep, send, part = project(
        place, gathered, hidden_all, target_all, right_local, projected, 32
    )

    near = lax.all_to_all(part, ("ylo", "core", "x", "yhi"), 0, 0, tiled=True)
    near = near.reshape(2, 2, 8, 2 * members).sum(axis=(0, 2)).reshape(1, 1, 4 * members)
    reward = lax.all_to_all(jnp.broadcast_to(near, (16, 1, 4 * members)), "z", 0, 0, tiled=True)
    recv = lax.ppermute(send, "ylo", SWAP)
    up_out = order(keep, recv, axis=1)
    step, fitness = step_product(place, reward, left_all, right_own, right_other, members)
    return (up_out, step, fitness.reshape(members))


def solution(mesh):
    fine = Mesh(mesh.devices.reshape(SIZES), AXES)
    pop = ("ylo", "z", "core")
    shard = ("x", "yhi")
    in_specs = (P(pop, None), P(pop, shard), P(pop, None), P(pop, shard), P(pop, shard))
    out_specs = (P(pop, shard), P(pop, shard), P(pop))
    return jax.shard_map(local, mesh=fine, in_specs=in_specs, out_specs=out_specs, check_vma=False)
```

```python
import math

import jax
import jax.numpy as jnp
from jax import lax
from jax.experimental import pallas as pl
from jax.experimental.pallas import tpu as pltpu
from jax.sharding import Mesh, PartitionSpec as P

noise_scale = 0.5
spread_eps = 1e-05
AXES = ("ylo", "z", "core", "x", "yhi")
SIZES = (2, 16, 2, 4, 2)
SWAP = [(0, 1), (1, 0)]


def project_kernel(
    place, gathered, hidden_hbm, target_hbm, right, projected, keep, send, reward, total, held, hidden, target, sems
):
    chunks, slabs, width, cols = held.shape
    rows = hidden.shape[0]
    members = right.shape[0]
    tokens = rows // members
    load_hidden = pltpu.make_async_copy(hidden_hbm, hidden, sems.at[0])
    load_hidden.start()
    copies = []
    for i in range(chunks):
        copy = pltpu.make_async_copy(
            gathered.at[pl.ds(i * slabs, slabs), pl.ds(0, width), :], held.at[i], sems.at[2 + i]
        )
        copy.start()
        copies.append(copy)
    load_target = pltpu.make_async_copy(target_hbm, target, sems.at[1])
    load_target.start()
    span = slabs * width
    load_hidden.wait()
    for i in range(chunks):
        copies[i].wait()
        part = jnp.dot(
            hidden[:, i * span : (i + 1) * span],
            held[i].reshape(span, cols),
            preferred_element_type=jnp.float32,
        )
        if i == 0:
            total[...] = part
        else:
            total[...] += part
    load_target.wait()
    scale = projected[...].reshape(members, tokens, 1)
    summed = jnp.zeros((members, 1), jnp.float32)
    for at in range(0, cols, 128):
        base = total[:, at : at + 128].reshape(members, tokens, 128)
        factor = right[:, at : at + 128].astype(jnp.float32)
        value = base + scale * factor[:, None, :]
        up = value.reshape(rows, 128).astype(jnp.bfloat16)
        keep[:, at : at + 128] = up[: rows // 2]
        send[:, at : at + 128] = up[rows // 2 :]
        aim = target[:, at : at + 128].astype(jnp.float32).reshape(members, tokens, 128)
        gain = value * (0.5 + 0.5 * jnp.tanh(0.5 * value)) * aim
        summed += jnp.sum(jnp.sum(gain, axis=1), axis=-1, keepdims=True)
    shape = (members, reward.shape[-1])
    row = lax.broadcasted_iota(jnp.int32, shape, 0) + place[0] * (members // 2)
    row = jnp.where(row < members, row, row - members)
    spot = row == lax.broadcasted_iota(jnp.int32, shape, 1)
    line = jnp.sum(jnp.where(spot, summed, 0.0), axis=0, keepdims=True)
    reward[...] = jnp.broadcast_to(line[None], reward.shape)


VMEM = pl.BlockSpec(memory_space=pltpu.VMEM)
SMEM = pl.BlockSpec(memory_space=pltpu.SMEM)
ANY = pl.BlockSpec(memory_space=pl.ANY)


def project(place, gathered, hidden, target, right, projected, peers):
    blocks, _, cols = gathered.shape
    rows, features = hidden.shape
    members = right.shape[0]
    width = features // blocks
    slabs = blocks // 8
    return pl.pallas_call(
        project_kernel,
        in_specs=[SMEM, ANY, ANY, ANY, VMEM, VMEM],
        out_specs=[VMEM, VMEM, VMEM],
        out_shape=[
            jax.ShapeDtypeStruct((rows // 2, cols), jnp.bfloat16),
            jax.ShapeDtypeStruct((rows // 2, cols), jnp.bfloat16),
            jax.ShapeDtypeStruct((peers, 1, members), jnp.float32),
        ],
        scratch_shapes=[
            pltpu.VMEM((rows, cols), jnp.float32),
            pltpu.VMEM((blocks // slabs, slabs, width, cols), jnp.bfloat16),
            pltpu.VMEM(hidden.shape, jnp.bfloat16),
            pltpu.VMEM(target.shape, jnp.bfloat16),
            pltpu.SemaphoreType.DMA((blocks // slabs + 2,)),
        ],
        compiler_params=pltpu.CompilerParams(vmem_limit_bytes=53 * 1024 * 1024),
        cost_estimate=pl.CostEstimate(
            flops=2 * rows * features * cols,
            bytes_accessed=features * cols * 2,
            transcendentals=rows * cols,
        ),
    )(place, gathered, hidden, target, right, projected)


def step_kernel(place, reward, left, right_own, right_other, out, fitness):
    members, depth = left.shape
    blocks, _, lanes = reward.shape
    value = reward[...].reshape(blocks, lanes)
    total = jnp.sum(jnp.sum(value, axis=0, keepdims=True), axis=1, keepdims=True)
    centered = value - total * (1.0 / members)
    squares = jnp.sum(jnp.sum(centered * centered, axis=0, keepdims=True), axis=1, keepdims=True)
    score = centered / jnp.sqrt(squares * (1.0 / members) + spread_eps)
    run = fitness.shape[1]
    shape = (blocks, lanes // 2, lanes)
    index = lax.broadcasted_iota(jnp.int32, shape, 1)
    lane = lax.broadcasted_iota(jnp.int32, shape, 2)
    columns = []
    for side in (place[0], 1 - place[0]):
        spot = lane == index + jnp.where(index < run, 0, run) + side * run
        column = jnp.sum(jnp.where(spot, score[:, None, :], 0.0), axis=-1, keepdims=True)
        columns.append(column.reshape(members // 2, 1))
    pick = (members // 2, run)
    mine = lax.broadcasted_iota(jnp.int32, pick, 0) == (
        lax.broadcasted_iota(jnp.int32, pick, 1) + place[1]
    )
    fitness[...] = jnp.sum(jnp.where(mine, columns[0], 0.0), axis=0, keepdims=True)
    both = []
    for side, column in enumerate(columns):
        rows = left[side * (members // 2) : (side + 1) * (members // 2)]
        weighted = rows.astype(jnp.float32) * column
        high = weighted.astype(jnp.bfloat16)
        low = (weighted - high.astype(jnp.float32)).astype(jnp.bfloat16)
        both.append(jnp.concatenate([high, low], axis=1))
    cols = right_own.shape[1]
    for at in range(0, cols, cols // 2):
        product = sum(
            lax.dot_general(
                factor,
                right[:, at : at + cols // 2],
                (((0,), (0,)), ((), ())),
                preferred_element_type=jnp.float32,
            )
            for factor, right in zip(both, (right_own, right_other))
        )
        out[:, at : at + cols // 2] = (product[:depth] + product[depth:]) * (
            1.0 / math.sqrt(members)
        )


def step_product(place, reward, left, right_own, right_other, own):
    members, depth = left.shape
    cols = right_own.shape[1]
    return pl.pallas_call(
        step_kernel,
        in_specs=[SMEM, VMEM, VMEM, VMEM, VMEM],
        out_specs=[VMEM, VMEM],
        out_shape=[
            jax.ShapeDtypeStruct((depth, cols), jnp.float32),
            jax.ShapeDtypeStruct((1, own), jnp.float32),
        ],
        compiler_params=pltpu.CompilerParams(vmem_limit_bytes=24 * 1024 * 1024),
        cost_estimate=pl.CostEstimate(
            flops=128 * depth * members * cols,
            bytes_accessed=members * cols * 4 + depth * cols * 4,
            transcendentals=0,
        ),
    )(place, reward, left, right_own, right_other)


def local(hidden, weight, left_factors, right_factors, target):
    members, features = left_factors.shape
    rows = hidden.shape[0]
    tokens = rows // members
    depth, cols = weight.shape
    half = cols // 2
    ylo = lax.axis_index("ylo")
    z = lax.axis_index("z")
    core = lax.axis_index("core")
    low = ylo == 0

    def own(a):
        return jnp.where(low, a[:, :half], a[:, half:])

    def other(a):
        return jnp.where(low, a[:, half:], a[:, :half])

    def order(a, b, axis=0):
        return jnp.where(
            low, jnp.concatenate([a, b], axis=axis), jnp.concatenate([b, a], axis=axis)
        )

    weight_recv = lax.ppermute(other(weight), "ylo", SWAP)
    packed = order(own(weight), weight_recv)
    gathered = lax.all_gather(packed, ("z", "core"), axis=0, tiled=False)

    _, hidden_b, left_b, target_b, right_b = lax.optimization_barrier(
        (packed, hidden, left_factors, target, right_factors)
    )
    right_own = lax.all_gather(right_b, ("z", "core"), axis=0, tiled=True)
    right_recv = lax.ppermute(other(right_b), "ylo", SWAP)
    right_local = jnp.concatenate([own(right_b), right_recv], axis=0)
    rows_recv = lax.ppermute(hidden_b, "ylo", SWAP)
    right_own, left_late, rows_recv = lax.optimization_barrier((right_own, left_b, rows_recv))
    right_other = lax.ppermute(right_own, "ylo", SWAP)
    target_recv = lax.ppermute(other(target_b), "ylo", SWAP)
    projected_own = (
        jnp.einsum(
            "mtd,md->mt",
            hidden_b.reshape(members, tokens, features),
            left_b,
            preferred_element_type=jnp.float32,
        ).reshape(rows, 1)
        * (noise_scale / math.sqrt(features))
    )
    projected_recv = lax.ppermute(projected_own, "ylo", SWAP)
    projected = jnp.concatenate([projected_own, projected_recv], axis=0)
    target_all = jnp.concatenate([own(target_b), target_recv], axis=0)
    hidden_all = jnp.concatenate([hidden_b, rows_recv], axis=0)
    spread_rows = hidden_all.reshape(2 * rows, 2, features // (2 * depth), depth)
    hidden_all = spread_rows.transpose(0, 2, 1, 3).reshape(2 * rows, features)

    left_split = left_late.reshape(members, features // depth, depth).transpose(1, 0, 2)
    left_all = lax.all_to_all(left_split, ("ylo", "z", "core"), 0, 0, tiled=True)
    left_all = left_all.reshape(2, features // (2 * depth), members, depth)
    left_all = jnp.where(low, left_all, left_all[::-1]).reshape(-1, depth)
    hidden_all, left_all, right_own, right_other = lax.optimization_barrier(
        (hidden_all, left_all, right_own, right_other)
    )
    place = jnp.stack([ylo, z * 2 * members + core * members]).astype(jnp.int32)
    keep, send, part = project(
        place, gathered, hidden_all, target_all, right_local, projected, 32
    )

    near = lax.all_to_all(part, ("ylo", "core", "x", "yhi"), 0, 0, tiled=True)
    near = near.reshape(2, 2, 8, 2 * members).sum(axis=(0, 2)).reshape(1, 1, 4 * members)
    reward = lax.all_to_all(jnp.broadcast_to(near, (16, 1, 4 * members)), "z", 0, 0, tiled=True)
    recv = lax.ppermute(send, "ylo", SWAP)
    up_out = order(keep, recv, axis=1)
    step, fitness = step_product(place, reward, left_all, right_own, right_other, members)
    return (up_out, step, fitness.reshape(members))


def solution(mesh):
    fine = Mesh(mesh.devices.reshape(SIZES), AXES)
    pop = ("ylo", "z", "core")
    shard = ("x", "yhi")
    in_specs = (P(pop, None), P(pop, shard), P(pop, None), P(pop, shard), P(pop, shard))
    out_specs = (P(pop, shard), P(pop, shard), P(pop))
    return jax.shard_map(local, mesh=fine, in_specs=in_specs, out_specs=out_specs, check_vma=False)
```

```python
import math

import jax
import jax.numpy as jnp
from jax import lax
from jax.experimental import pallas as pl
from jax.experimental.pallas import tpu as pltpu
from jax.sharding import Mesh, PartitionSpec as P

noise_scale = 0.5
spread_eps = 1e-05
AXES = ("ylo", "z", "core", "x", "yhi")
SIZES = (2, 16, 2, 4, 2)
SWAP = [(0, 1), (1, 0)]


def project_kernel(
    place, gathered, hidden_hbm, target_hbm, right, projected, keep, send, reward, total, held, hidden, target, sems
):
    chunks, slabs, width, cols = held.shape
    rows = hidden.shape[0]
    members = right.shape[0]
    tokens = rows // members
    load_hidden = pltpu.make_async_copy(hidden_hbm, hidden, sems.at[0])
    load_hidden.start()
    copies = []
    for i in range(chunks):
        copy = pltpu.make_async_copy(
            gathered.at[pl.ds(i * slabs, slabs), pl.ds(0, width), :], held.at[i], sems.at[2 + i]
        )
        copy.start()
        copies.append(copy)
    load_target = pltpu.make_async_copy(target_hbm, target, sems.at[1])
    load_target.start()
    span = slabs * width
    load_hidden.wait()
    for i in range(chunks):
        copies[i].wait()
        part = jnp.dot(
            hidden[:, i * span : (i + 1) * span],
            held[i].reshape(span, cols),
            preferred_element_type=jnp.float32,
        )
        if i == 0:
            total[...] = part
        else:
            total[...] += part
    load_target.wait()
    scale = projected[...].reshape(members, tokens, 1)
    summed = jnp.zeros((members, 1), jnp.float32)
    for at in range(0, cols, 128):
        base = total[:, at : at + 128].reshape(members, tokens, 128)
        factor = right[:, at : at + 128].astype(jnp.float32)
        value = base + scale * factor[:, None, :]
        up = value.reshape(rows, 128).astype(jnp.bfloat16)
        keep[:, at : at + 128] = up[: rows // 2]
        send[:, at : at + 128] = up[rows // 2 :]
        aim = target[:, at : at + 128].astype(jnp.float32).reshape(members, tokens, 128)
        gain = value * (0.5 + 0.5 * jnp.tanh(0.5 * value)) * aim
        summed += jnp.sum(jnp.sum(gain, axis=1), axis=-1, keepdims=True)
    shape = (members, reward.shape[-1])
    row = lax.broadcasted_iota(jnp.int32, shape, 0) + place[0] * (members // 2)
    row = jnp.where(row < members, row, row - members)
    spot = row == lax.broadcasted_iota(jnp.int32, shape, 1)
    line = jnp.sum(jnp.where(spot, summed, 0.0), axis=0, keepdims=True)
    reward[...] = jnp.broadcast_to(line[None], reward.shape)


VMEM = pl.BlockSpec(memory_space=pltpu.VMEM)
SMEM = pl.BlockSpec(memory_space=pltpu.SMEM)
ANY = pl.BlockSpec(memory_space=pl.ANY)


def project(place, gathered, hidden, target, right, projected, peers):
    blocks, _, cols = gathered.shape
    rows, features = hidden.shape
    members = right.shape[0]
    width = features // blocks
    slabs = blocks // 4
    return pl.pallas_call(
        project_kernel,
        in_specs=[SMEM, ANY, ANY, ANY, VMEM, VMEM],
        out_specs=[VMEM, VMEM, VMEM],
        out_shape=[
            jax.ShapeDtypeStruct((rows // 2, cols), jnp.bfloat16),
            jax.ShapeDtypeStruct((rows // 2, cols), jnp.bfloat16),
            jax.ShapeDtypeStruct((peers, 1, members), jnp.float32),
        ],
        scratch_shapes=[
            pltpu.VMEM((rows, cols), jnp.float32),
            pltpu.VMEM((blocks // slabs, slabs, width, cols), jnp.bfloat16),
            pltpu.VMEM(hidden.shape, jnp.bfloat16),
            pltpu.VMEM(target.shape, jnp.bfloat16),
            pltpu.SemaphoreType.DMA((blocks // slabs + 2,)),
        ],
        compiler_params=pltpu.CompilerParams(vmem_limit_bytes=53 * 1024 * 1024),
        cost_estimate=pl.CostEstimate(
            flops=2 * rows * features * cols,
            bytes_accessed=features * cols * 2,
            transcendentals=rows * cols,
        ),
    )(place, gathered, hidden, target, right, projected)


def step_kernel(place, reward, left, right_own, right_other, out, fitness):
    members, depth = left.shape
    blocks, _, lanes = reward.shape
    value = reward[...].reshape(blocks, lanes)
    total = jnp.sum(jnp.sum(value, axis=0, keepdims=True), axis=1, keepdims=True)
    centered = value - total * (1.0 / members)
    squares = jnp.sum(jnp.sum(centered * centered, axis=0, keepdims=True), axis=1, keepdims=True)
    score = centered / jnp.sqrt(squares * (1.0 / members) + spread_eps)
    run = fitness.shape[1]
    shape = (blocks, lanes // 2, lanes)
    index = lax.broadcasted_iota(jnp.int32, shape, 1)
    lane = lax.broadcasted_iota(jnp.int32, shape, 2)
    columns = []
    for side in (place[0], 1 - place[0]):
        spot = lane == index + jnp.where(index < run, 0, run) + side * run
        column = jnp.sum(jnp.where(spot, score[:, None, :], 0.0), axis=-1, keepdims=True)
        columns.append(column.reshape(members // 2, 1))
    pick = (members // 2, run)
    mine = lax.broadcasted_iota(jnp.int32, pick, 0) == (
        lax.broadcasted_iota(jnp.int32, pick, 1) + place[1]
    )
    fitness[...] = jnp.sum(jnp.where(mine, columns[0], 0.0), axis=0, keepdims=True)
    both = []
    for side, column in enumerate(columns):
        rows = left[side * (members // 2) : (side + 1) * (members // 2)]
        weighted = rows.astype(jnp.float32) * column
        high = weighted.astype(jnp.bfloat16)
        low = (weighted - high.astype(jnp.float32)).astype(jnp.bfloat16)
        both.append(jnp.concatenate([high, low], axis=1))
    cols = right_own.shape[1]
    for at in range(0, cols, cols // 2):
        product = sum(
            lax.dot_general(
                factor,
                right[:, at : at + cols // 2],
                (((0,), (0,)), ((), ())),
                preferred_element_type=jnp.float32,
            )
            for factor, right in zip(both, (right_own, right_other))
        )
        out[:, at : at + cols // 2] = (product[:depth] + product[depth:]) * (
            1.0 / math.sqrt(members)
        )


def step_product(place, reward, left, right_own, right_other, own):
    members, depth = left.shape
    cols = right_own.shape[1]
    return pl.pallas_call(
        step_kernel,
        in_specs=[SMEM, VMEM, VMEM, VMEM, VMEM],
        out_specs=[VMEM, VMEM],
        out_shape=[
            jax.ShapeDtypeStruct((depth, cols), jnp.float32),
            jax.ShapeDtypeStruct((1, own), jnp.float32),
        ],
        compiler_params=pltpu.CompilerParams(vmem_limit_bytes=24 * 1024 * 1024),
        cost_estimate=pl.CostEstimate(
            flops=128 * depth * members * cols,
            bytes_accessed=members * cols * 4 + depth * cols * 4,
            transcendentals=0,
        ),
    )(place, reward, left, right_own, right_other)


def local(hidden, weight, left_factors, right_factors, target):
    members, features = left_factors.shape
    rows = hidden.shape[0]
    tokens = rows // members
    depth, cols = weight.shape
    half = cols // 2
    ylo = lax.axis_index("ylo")
    z = lax.axis_index("z")
    core = lax.axis_index("core")
    low = ylo == 0

    def own(a):
        return jnp.where(low, a[:, :half], a[:, half:])

    def other(a):
        return jnp.where(low, a[:, half:], a[:, :half])

    def order(a, b, axis=0):
        return jnp.where(
            low, jnp.concatenate([a, b], axis=axis), jnp.concatenate([b, a], axis=axis)
        )

    weight_recv = lax.ppermute(other(weight), "ylo", SWAP)
    packed = order(own(weight), weight_recv)
    gathered = lax.all_gather(packed, ("z", "core"), axis=0, tiled=False)

    _, hidden_b, left_b, target_b, right_b = lax.optimization_barrier(
        (packed, hidden, left_factors, target, right_factors)
    )
    right_own = lax.all_gather(right_b, ("z", "core"), axis=0, tiled=True)
    right_other = lax.ppermute(right_own, "ylo", SWAP)
    right_recv = lax.ppermute(other(right_b), "ylo", SWAP)
    right_local = jnp.concatenate([own(right_b), right_recv], axis=0)
    rows_recv = lax.ppermute(hidden_b, "ylo", SWAP)
    target_recv = lax.ppermute(other(target_b), "ylo", SWAP)
    projected_own = (
        jnp.einsum(
            "mtd,md->mt",
            hidden_b.reshape(members, tokens, features),
            left_b,
            preferred_element_type=jnp.float32,
        ).reshape(rows, 1)
        * (noise_scale / math.sqrt(features))
    )
    projected_recv = lax.ppermute(projected_own, "ylo", SWAP)
    projected = jnp.concatenate([projected_own, projected_recv], axis=0)
    target_all = jnp.concatenate([own(target_b), target_recv], axis=0)
    hidden_all = jnp.concatenate([hidden_b, rows_recv], axis=0)
    spread_rows = hidden_all.reshape(2 * rows, 2, features // (2 * depth), depth)
    hidden_all = spread_rows.transpose(0, 2, 1, 3).reshape(2 * rows, features)

    left_split = left_b.reshape(members, features // depth, depth).transpose(1, 0, 2)
    left_all = lax.all_to_all(left_split, ("ylo", "z", "core"), 0, 0, tiled=True)
    left_all = left_all.reshape(2, features // (2 * depth), members, depth)
    left_all = jnp.where(low, left_all, left_all[::-1]).reshape(-1, depth)
    hidden_all, left_all, right_own = lax.optimization_barrier((hidden_all, left_all, right_own))
    place = jnp.stack([ylo, z * 2 * members + core * members]).astype(jnp.int32)
    keep, send, part = project(
        place, gathered, hidden_all, target_all, right_local, projected, 32
    )

    near = lax.all_to_all(part, ("ylo", "core", "x", "yhi"), 0, 0, tiled=True)
    near = near.reshape(2, 2, 8, 2 * members).sum(axis=(0, 2)).reshape(1, 1, 4 * members)
    reward = lax.all_to_all(jnp.broadcast_to(near, (16, 1, 4 * members)), "z", 0, 0, tiled=True)
    recv = lax.ppermute(send, "ylo", SWAP)
    up_out = order(keep, recv, axis=1)
    step, fitness = step_product(place, reward, left_all, right_own, right_other, members)
    return (up_out, step, fitness.reshape(members))


def solution(mesh):
    fine = Mesh(mesh.devices.reshape(SIZES), AXES)
    pop = ("ylo", "z", "core")
    shard = ("x", "yhi")
    in_specs = (P(pop, None), P(pop, shard), P(pop, None), P(pop, shard), P(pop, shard))
    out_specs = (P(pop, shard), P(pop, shard), P(pop))
    return jax.shard_map(local, mesh=fine, in_specs=in_specs, out_specs=out_specs, check_vma=False)
```
